32 devices in a mesh: slab: 16 (over z, y, x), grp: 2 (over core).
Axes of the slice: x: 2, y: 2, z: 4, core: 2. Of those that a mesh axis runs over, the one named last changes fastest.
Arguments:
- echo_data: bfloat16 [16, 1024, 2048], P('slab', 'grp'), may hold values from -6 to 6
- acquirer: int32 [3], replicated, may hold values from 0 to 15, as said below
- panels: bfloat16 [16, 3, 64, 128, 128], P('slab', None, 'grp'), may hold values from -0.00390625 to 0.00390625
- block_count: int32 [16, 3], P('slab'), may hold values from 16 to 64, as said below
- block_rows: int32 [16, 3, 64], P('slab'), may hold values from 0 to 7
- block_columns: int32 [16, 3, 64], P('slab'), may hold values from 0 to 15
- apodization: float32 [16, 1024], P(None, 'grp'), may hold values from 0.25 to 2.5
- window_index: int32 [16384], P('slab'), may hold values from 0 to 15
Outputs:
- image: float32 [16384], P(('slab', 'grp'))
The draws below stay inside these ranges and needn't reach their ends.
Inputs may be any that keep to these rules, and one draw needn't show every extreme that they name: `acquirer`: 3 distinct slab indices, the last slab index always among them. `block_count`: slots below the count are live, the others unused; some slab and transmit has all 64 live in every draw.
All inputs are finite; a program needn't handle non-finite values.
Results may differ from the reference program's by a relative error of at most 0.0003.
Values may be sent and summed in bfloat16 or wider, within the bound.
A program may use at most 128 MiB of HBM per device.

```python
import math
import jax
import jax.numpy as jnp
from jax import lax

CHAN = 1024
SAMPLES = 2048
BLK = 128
TX = 3
NWIN = 16
RB = 8
SB = 16
NB = 64
VOX_SLAB = 1024
VOXELS = 16384
N_SLAB = 16


def draw_acquirer(key, part):
    others = jax.random.permutation(jax.random.fold_in(key, 3), N_SLAB - 1)[:TX - 1]
    values = jnp.concatenate([others.astype(jnp.int32), jnp.full((1,), N_SLAB - 1, jnp.int32)])
    order = jax.random.permutation(jax.random.fold_in(key, 4), TX)
    return values[order].astype(jnp.int32)


def draw_block_count(key, part):
    counts_drawn = jax.random.randint(jax.random.fold_in(key, 1), (N_SLAB, TX), NB // 4, NB + 1)
    busiest = jax.random.randint(jax.random.fold_in(key, 2), (), 0, N_SLAB)
    return counts_drawn.at[busiest, 0].set(NB).astype(jnp.int32)


def with_ends(result, own_key, low, top_value):
    extent = result.shape
    spot = [jax.random.randint(jax.random.fold_in(own_key, axis), (), 0, extent[axis]) for axis in range(len(extent))]
    result = result.at[tuple(spot)].set(low)
    longest = extent.index(max(extent))
    spot[longest] = (spot[longest] + 1) % extent[longest]
    return result.at[tuple(spot)].set(top_value)


def shard_levels(stream_key, shape, cuts, least, top_value):
    gain, own = 1.0, jax.random.fold_in(stream_key, 6)
    for dim, blocks in cuts:
        steps = jnp.exp(jax.random.uniform(jax.random.fold_in(own, dim), (blocks,), jnp.float32, least / len(cuts), top_value / len(cuts)))
        gain = gain * jnp.repeat(steps, shape[dim] // blocks).reshape([-1 if axis == dim else 1 for axis in range(len(shape))])
    return gain


def centred(rng, shape, scale, bound, cuts=(), held_as=jnp.bfloat16):
    gain = shard_levels(rng, shape, cuts, -0.22, 0.18) if cuts else 1.0
    entries = jax.random.normal(rng, shape, jnp.float32) * scale * gain
    return jnp.minimum(jnp.maximum(entries, -bound), bound).astype(held_as)


def setup_inputs(seed: int = 0) -> dict:
    keys = jax.random.split(jax.random.key(seed), 9)
    echo_data = centred(keys[0], (N_SLAB, CHAN, SAMPLES), 1.0, 6.0, ((0, 16), (1, 2)))
    acquirer = draw_acquirer(jax.random.fold_in(keys[8], 71), 0)
    panels = centred(keys[2], (N_SLAB, TX, NB, BLK, BLK), (BLK * CHAN * 16) ** -0.5, 0.00390625, ((0, 16), (2, 2)))
    block_count = draw_block_count(jax.random.fold_in(keys[8], 71), 0)
    block_rows = with_ends(jax.random.randint(keys[4], (N_SLAB, TX, NB), 0, RB), jax.random.fold_in(keys[4], 1), 0, RB - 1).astype(jnp.int32)
    block_columns = with_ends(jax.random.randint(keys[5], (N_SLAB, TX, NB), 0, SB), jax.random.fold_in(keys[5], 1), 0, SB - 1).astype(jnp.int32)
    apodization = jnp.clip(jnp.exp(math.log(2.5) - 2.3025851 * jax.random.uniform(keys[6], (NWIN, CHAN), jnp.float32) ** shard_levels(keys[6], (NWIN, CHAN), ((1, 2),), -0.2, 0.2)), 0.25, 2.5)
    window_index = with_ends(jax.random.randint(keys[7], (VOXELS,), 0, NWIN), jax.random.fold_in(keys[7], 1), 0, NWIN - 1).astype(jnp.int32)
    return dict(echo_data=echo_data, acquirer=acquirer, panels=panels, block_count=block_count, block_rows=block_rows, block_columns=block_columns, apodization=apodization, window_index=window_index)


def reference(echo_data, acquirer, panels, block_count, block_rows, block_columns, apodization, window_index):
    grids = [echo_data[acquirer[transmit]].reshape(CHAN, SB, BLK) for transmit in range(TX)]

    def slab_image(inputs):
        slab_panels, slab_counts, slab_rows, slab_columns, slab_windows = inputs
        running = jnp.zeros((RB, BLK, CHAN), jnp.float32)
        for transmit in range(TX):
            picked = jnp.take(grids[transmit], slab_columns[transmit].astype(jnp.int32), axis=1)
            terms = jnp.einsum("kvs,cks->kvc", slab_panels[transmit].astype(jnp.float32), picked.astype(jnp.float32))
            live = (jnp.arange(NB, dtype=jnp.int32) < slab_counts[transmit]).astype(jnp.float32)
            onehot = (slab_rows[transmit][:, None] == jnp.arange(RB, dtype=jnp.int32)[None, :]).astype(jnp.float32) * live[:, None]
            running = running + jnp.einsum("kr,kvc->rvc", onehot, terms, precision=lax.Precision.HIGHEST)
        weights = jnp.take(apodization, slab_windows.astype(jnp.int32), axis=0)
        return jnp.sum(running.reshape(VOX_SLAB, CHAN) * weights, axis=1)

    slabs = lax.map(slab_image, (panels, block_count, block_rows, block_columns, window_index.reshape(N_SLAB, VOX_SLAB)))
    return slabs.reshape(VOXELS)
```

```python
import functools

import jax
import jax.numpy as jnp
from jax import lax
from jax.experimental import pallas as pl
from jax.experimental.pallas import tpu as pltpu
from jax.sharding import PartitionSpec as P

MESH = pl.DeviceIdType.MESH
F32 = jnp.float32
BF16 = jnp.bfloat16
LANES = 128


def split_terms(x, n):
    terms = []
    for _ in range(n):
        term = x.astype(BF16)
        terms.append(term)
        x = x - term.astype(F32)
    return terms


def kernel(
    dims,
    echo,
    panels,
    apod,
    windows,
    acquirer,
    counts,
    rows,
    columns,
    image,
    echo_v,
    panels_v,
    own,
    parts,
    line,
    table,
    onehot,
    sums,
    echo_sem,
    panel_sem,
    send1,
    recv1,
    send2,
    recv2,
    send3,
    recv3,
    send4,
    recv4,
):
    n_grp, plane, n_lines, n_tx, n_win, piece, width, unroll = dims
    peers = plane * n_grp
    span = piece * LANES
    slab, grp = lax.axis_index("slab"), lax.axis_index("grp")
    level, spot = slab // plane, slab % plane
    me = spot * n_grp + grp

    def peer(step):
        other = lax.rem(me + step, peers)
        return other, (level * plane + other // n_grp, lax.rem(other, n_grp))

    def along(step):
        other = lax.rem(level + step, n_lines)
        return other, (other * plane + spot, grp)

    def sibling(step):
        other = lax.rem(grp + step, n_grp)
        return other, (slab, other)

    barrier = pltpu.get_barrier_semaphore()
    for step in range(1, peers):
        pl.semaphore_signal(barrier, inc=1, device_id=peer(step)[1], device_id_type=MESH)
    for step in range(1, n_lines):
        pl.semaphore_signal(barrier, inc=1, device_id=along(step)[1], device_id_type=MESH)

    order = [lax.rem(me + step, peers) for step in range(1, peers + 1)]
    loads = []
    for number, part in enumerate(order):
        cut = pl.ds(pl.multiple_of(part * span, span), span)
        load = pltpu.make_async_copy(echo.at[0, :, cut], echo_v.at[number], echo_sem.at[number])
        load.start()
        loads.append(load)
    panel_loads = []
    for t in range(n_tx):
        load = pltpu.make_async_copy(panels.at[0, t], panels_v.at[t], panel_sem.at[t])
        load.start()
        panel_loads.append(load)

    row_blocks = windows.shape[0]
    for r in range(row_blocks):
        ids = lax.broadcasted_iota(jnp.int32, (n_win, LANES), 0)
        onehot[r] = jnp.where(ids == windows[r : r + 1, :], 1.0, 0.0).astype(F32)

    weights = jnp.concatenate(split_terms(apod[...], 3), axis=0)

    pl.semaphore_wait(barrier, peers - 1 + n_lines - 1)

    copies = []
    for number, part in enumerate(order):
        loads[number].wait()
        terms = jnp.dot(weights, echo_v[number], preferred_element_type=F32)
        value = terms[:n_win] + terms[n_win : 2 * n_win] + terms[2 * n_win :]
        for c in range(piece):
            chunk = value[:, c * LANES : (c + 1) * LANES]
            if number == peers - 1:
                parts[me, c] = chunk
            else:
                own[number, c] = chunk
        if number < peers - 1:
            copy = pltpu.make_async_remote_copy(
                src_ref=own.at[number],
                dst_ref=parts.at[me],
                send_sem=send1.at[number],
                recv_sem=recv1.at[me],
                device_id=peer(number + 1)[1],
                device_id_type=MESH,
            )
            copy.start()
            copies.append(copy)
    for step in range(1, peers):
        other, place = peer(step)
        pltpu.make_async_remote_copy(
            src_ref=own.at[0],
            dst_ref=parts.at[other],
            send_sem=send1.at[0],
            recv_sem=recv1.at[other],
            device_id=place,
            device_id_type=MESH,
        ).wait_recv()

    for c in range(piece):
        records = []
        for q in range(plane):
            total = parts[q * n_grp, c]
            for g in range(1, n_grp):
                total = total + parts[q * n_grp + g, c]
            records.append(total)
        for t in range(n_tx):
            value = jnp.zeros((n_win, LANES), F32)
            for q in range(plane):
                hit = jnp.full((n_win, LANES), acquirer[t], jnp.int32) == level * plane + q
                value = value + jnp.where(hit, records[q], 0.0)
            line[level, c, t] = value
    for step in range(1, n_lines):
        other, place = along(step)
        copy = pltpu.make_async_remote_copy(
            src_ref=line.at[level],
            dst_ref=line.at[level],
            send_sem=send2.at[step],
            recv_sem=recv2.at[level],
            device_id=place,
            device_id_type=MESH,
        )
        copy.start()
        copies.append(copy)
    for step in range(1, n_lines):
        other, place = along(step)
        pltpu.make_async_remote_copy(
            src_ref=line.at[other],
            dst_ref=line.at[other],
            send_sem=send2.at[step],
            recv_sem=recv2.at[other],
            device_id=place,
            device_id_type=MESH,
        ).wait_recv()

    mine = pl.ds(me * piece, piece)
    for c in range(piece):
        for t in range(n_tx):
            value = line[0, c, t]
            for l in range(1, n_lines):
                value = value + line[l, c, t]
            table[me * piece + c, t] = jnp.concatenate(split_terms(value, 2), axis=0)
    for step in range(1, peers):
        other, place = peer(step)
        copy = pltpu.make_async_remote_copy(
            src_ref=table.at[mine],
            dst_ref=table.at[mine],
            send_sem=send3.at[step],
            recv_sem=recv3.at[me],
            device_id=place,
            device_id_type=MESH,
        )
        copy.start()
        copies.append(copy)
    for step in range(1, peers):
        other, place = peer(step)
        theirs = pl.ds(other * piece, piece)
        pltpu.make_async_remote_copy(
            src_ref=table.at[theirs],
            dst_ref=table.at[theirs],
            send_sem=send3.at[step],
            recv_sem=recv3.at[other],
            device_id=place,
            device_id_type=MESH,
        ).wait_recv()

    row_ids = lax.broadcasted_iota(jnp.int32, (row_blocks, LANES), 0)
    acc = jnp.zeros((row_blocks, LANES), F32)
    for t in range(n_tx):
        panel_loads[t].wait()

        def some_slots(turn, acc, t=t):
            for u in range(unroll):
                k = turn * unroll + u
                slot = grp * width + k
                r = rows[t, 0, slot]
                signal = table[columns[t, 0, slot], t]
                both = lax.dot_general(
                    signal,
                    panels_v[t, k],
                    (((1,), (1,)), ((), ())),
                    preferred_element_type=F32,
                )
                value = (both[:n_win] + both[n_win:]) * onehot[r]
                value = jnp.sum(value, axis=0, keepdims=True)
                target = jnp.where(slot < counts[0, t], r, -1)
                acc = acc + jnp.where(row_ids == target, value, 0.0)
            return acc

        acc = lax.fori_loop(0, width // unroll, some_slots, acc)

    sums[grp] = acc
    for step in range(1, n_grp):
        other, place = sibling(step)
        copy = pltpu.make_async_remote_copy(
            src_ref=sums.at[grp],
            dst_ref=sums.at[grp],
            send_sem=send4.at[step],
            recv_sem=recv4.at[grp],
            device_id=place,
            device_id_type=MESH,
        )
        copy.start()
        copies.append(copy)
    for step in range(1, n_grp):
        other, place = sibling(step)
        pltpu.make_async_remote_copy(
            src_ref=sums.at[other],
            dst_ref=sums.at[other],
            send_sem=send4.at[step],
            recv_sem=recv4.at[other],
            device_id=place,
            device_id_type=MESH,
        ).wait_recv()
    total = sums[0]
    for g in range(1, n_grp):
        total = total + sums[g]
    share = row_blocks // n_grp
    result = total[:share]
    for g in range(1, n_grp):
        result = jnp.where(grp == g, total[g * share : (g + 1) * share], result)
    image[...] = result
    for copy in copies:
        copy.wait_send()


def per_device(
    n_slab,
    n_grp,
    echo_data,
    acquirer,
    panels,
    block_count,
    block_rows,
    block_columns,
    apodization,
    window_index,
):
    channels, samples = echo_data.shape[1:]
    n_tx, width, block = panels.shape[1:4]
    n_win = apodization.shape[0]
    n_blocks = samples // block
    row_blocks = window_index.shape[0] // block
    plane = min(4, n_slab, n_blocks // n_grp)
    n_lines = n_slab // plane
    peers = plane * n_grp
    piece = n_blocks // peers
    assert block == LANES and piece * peers == n_blocks and plane * n_lines == n_slab
    unroll = min(8, width)
    dims = (n_grp, plane, n_lines, n_tx, n_win, piece, width, unroll)
    vmem = pl.BlockSpec(memory_space=pltpu.VMEM)
    smem = pl.BlockSpec(memory_space=pltpu.SMEM)
    hbm = pl.BlockSpec(memory_space=pltpu.HBM)
    dma = pltpu.SemaphoreType.DMA
    result = pl.pallas_call(
        functools.partial(kernel, dims),
        out_shape=jax.ShapeDtypeStruct((row_blocks // n_grp, LANES), F32),
        in_specs=[hbm, hbm, vmem, vmem, smem, smem, smem, smem],
        out_specs=vmem,
        scratch_shapes=[
            pltpu.VMEM((peers, channels, piece * LANES), BF16),
            pltpu.VMEM((n_tx, width, block, block), BF16),
            pltpu.VMEM((peers, piece, n_win, LANES), F32),
            pltpu.VMEM((peers, piece, n_win, LANES), F32),
            pltpu.VMEM((n_lines, piece, n_tx, n_win, LANES), F32),
            pltpu.VMEM((n_blocks, n_tx, 2 * n_win, LANES), BF16),
            pltpu.VMEM((row_blocks, n_win, LANES), F32),
            pltpu.VMEM((n_grp, row_blocks, LANES), F32),
            dma((peers,)),
            dma((n_tx,)),
            dma((peers,)),
            dma((peers,)),
            dma((n_lines,)),
            dma((n_lines,)),
            dma((peers,)),
            dma((peers,)),
            dma((n_grp,)),
            dma((n_grp,)),
        ],
        compiler_params=pltpu.CompilerParams(
            collective_id=0, has_side_effects=True, vmem_limit_bytes=62 * 1024 * 1024
        ),
        name="beamform",
    )(
        echo_data,
        panels,
        apodization,
        window_index.reshape(row_blocks, block),
        acquirer,
        block_count,
        block_rows.transpose(1, 0, 2),
        block_columns.transpose(1, 0, 2),
    )
    return result.reshape(-1)


def solution(mesh):
    return jax.shard_map(
        functools.partial(per_device, mesh.shape["slab"], mesh.shape["grp"]),
        mesh=mesh,
        in_specs=(
            P("slab", "grp", None),
            P(),
            P("slab", None, "grp", None, None),
            P("slab", None),
            P("slab", None, None),
            P("slab", None, None),
            P(None, "grp"),
            P("slab"),
        ),
        out_specs=P(("slab", "grp")),
        check_vma=False,
    )
```

```python
import functools

import jax
import jax.numpy as jnp
from jax import lax
from jax.experimental import pallas as pl
from jax.experimental.pallas import tpu as pltpu
from jax.sharding import PartitionSpec as P

MESH = pl.DeviceIdType.MESH
F32 = jnp.float32
BF16 = jnp.bfloat16
LANES = 128


def split_terms(x, n):
    terms = []
    for _ in range(n):
        term = x.astype(BF16)
        terms.append(term)
        x = x - term.astype(F32)
    return terms


def kernel(
    dims,
    echo,
    panels,
    apod,
    windows,
    acquirer,
    counts,
    rows,
    columns,
    image,
    echo_v,
    panels_v,
    own,
    parts,
    line,
    tables,
    onehot,
    sums,
    echo_sem,
    panel_sem,
    send1,
    recv1,
    send2,
    recv2,
    send3,
    recv3,
    send4,
    recv4,
):
    n_grp, plane, n_lines, n_tx, n_win, piece, width, unroll = dims
    peers = plane * n_grp
    span = piece * LANES
    slab, grp = lax.axis_index("slab"), lax.axis_index("grp")
    level, spot = slab // plane, slab % plane
    me = spot * n_grp + grp

    def peer(step):
        other = lax.rem(me + step, peers)
        return other, (level * plane + other // n_grp, lax.rem(other, n_grp))

    def along(step):
        other = lax.rem(level + step, n_lines)
        return other, (other * plane + spot, grp)

    def sibling(step):
        other = lax.rem(grp + step, n_grp)
        return other, (slab, other)

    barrier = pltpu.get_barrier_semaphore()
    for step in range(1, peers):
        pl.semaphore_signal(barrier, inc=1, device_id=peer(step)[1], device_id_type=MESH)
    for step in range(1, n_lines):
        pl.semaphore_signal(barrier, inc=1, device_id=along(step)[1], device_id_type=MESH)

    order = [lax.rem(me + step, peers) for step in range(1, peers + 1)]
    loads = []
    for number, part in enumerate(order):
        cut = pl.ds(pl.multiple_of(part * span, span), span)
        load = pltpu.make_async_copy(echo.at[0, :, cut], echo_v.at[number], echo_sem.at[number])
        load.start()
        loads.append(load)
    panel_loads = []
    for t in range(n_tx):
        load = pltpu.make_async_copy(panels.at[0, t], panels_v.at[t], panel_sem.at[t])
        load.start()
        panel_loads.append(load)

    row_blocks = windows.shape[0]
    for r in range(row_blocks):
        ids = lax.broadcasted_iota(jnp.int32, (n_win, LANES), 0)
        onehot[r] = jnp.where(ids == windows[r : r + 1, :], 1.0, 0.0).astype(F32)

    weights = jnp.concatenate(split_terms(apod[...], 3), axis=0)

    pl.semaphore_wait(barrier, peers - 1 + n_lines - 1)

    copies = []
    for number, part in enumerate(order):
        loads[number].wait()
        terms = jnp.dot(weights, echo_v[number], preferred_element_type=F32)
        value = terms[:n_win] + terms[n_win : 2 * n_win] + terms[2 * n_win :]
        for c in range(piece):
            chunk = value[:, c * LANES : (c + 1) * LANES]
            if number == peers - 1:
                parts[me, c] = chunk
            else:
                own[number, c] = chunk
        if number < peers - 1:
            copy = pltpu.make_async_remote_copy(
                src_ref=own.at[number],
                dst_ref=parts.at[me],
                send_sem=send1.at[number],
                recv_sem=recv1.at[me],
                device_id=peer(number + 1)[1],
                device_id_type=MESH,
            )
            copy.start()
            copies.append(copy)
    for step in range(1, peers):
        other, place = peer(step)
        pltpu.make_async_remote_copy(
            src_ref=own.at[0],
            dst_ref=parts.at[other],
            send_sem=send1.at[0],
            recv_sem=recv1.at[other],
            device_id=place,
            device_id_type=MESH,
        ).wait_recv()

    records = []
    for c in range(piece):
        for q in range(plane):
            total = parts[q * n_grp, c]
            for g in range(1, n_grp):
                total = total + parts[q * n_grp + g, c]
            records.append(total)
    for t in range(n_tx):
        for c in range(piece):
            value = jnp.zeros((n_win, LANES), F32)
            for q in range(plane):
                hit = jnp.full((n_win, LANES), acquirer[t], jnp.int32) == level * plane + q
                value = value + jnp.where(hit, records[c * plane + q], 0.0)
            line[level, t, c] = value
        for step in range(1, n_lines):
            other, place = along(step)
            copy = pltpu.make_async_remote_copy(
                src_ref=line.at[level, t],
                dst_ref=line.at[level, t],
                send_sem=send2.at[t, step],
                recv_sem=recv2.at[t, level],
                device_id=place,
                device_id_type=MESH,
            )
            copy.start()
            copies.append(copy)

    mine = pl.ds(me * piece, piece)
    for t in range(n_tx):
        for step in range(1, n_lines):
            other, place = along(step)
            pltpu.make_async_remote_copy(
                src_ref=line.at[other, t],
                dst_ref=line.at[other, t],
                send_sem=send2.at[t, step],
                recv_sem=recv2.at[t, other],
                device_id=place,
                device_id_type=MESH,
            ).wait_recv()
        for c in range(piece):
            value = line[0, t, c]
            for l in range(1, n_lines):
                value = value + line[l, t, c]
            tables[t][me * piece + c] = jnp.concatenate(split_terms(value, 2), axis=0)
        for step in range(1, peers):
            other, place = peer(step)
            copy = pltpu.make_async_remote_copy(
                src_ref=tables[t].at[mine],
                dst_ref=tables[t].at[mine],
                send_sem=send3.at[t, step],
                recv_sem=recv3.at[t, me],
                device_id=place,
                device_id_type=MESH,
            )
            copy.start()
            copies.append(copy)

    row_ids = lax.broadcasted_iota(jnp.int32, (row_blocks, LANES), 0)
    acc = jnp.zeros((row_blocks, LANES), F32)
    for t in range(n_tx):
        panel_loads[t].wait()
        for step in range(1, peers):
            other, place = peer(step)
            theirs = pl.ds(other * piece, piece)
            pltpu.make_async_remote_copy(
                src_ref=tables[t].at[theirs],
                dst_ref=tables[t].at[theirs],
                send_sem=send3.at[t, step],
                recv_sem=recv3.at[t, other],
                device_id=place,
                device_id_type=MESH,
            ).wait_recv()

        def some_slots(turn, acc, t=t):
            for u in range(unroll):
                k = turn * unroll + u
                slot = grp * width + k
                r = rows[t, 0, slot]
                signal = tables[t][columns[t, 0, slot]]
                both = lax.dot_general(
                    signal,
                    panels_v[t, k],
                    (((1,), (1,)), ((), ())),
                    preferred_element_type=F32,
                )
                value = (both[:n_win] + both[n_win:]) * onehot[r]
                value = jnp.sum(value, axis=0, keepdims=True)
                target = jnp.where(slot < counts[0, t], r, -1)
                acc = acc + jnp.where(row_ids == target, value, 0.0)
            return acc

        acc = lax.fori_loop(0, width // unroll, some_slots, acc)

    sums[grp] = acc
    for step in range(1, n_grp):
        other, place = sibling(step)
        copy = pltpu.make_async_remote_copy(
            src_ref=sums.at[grp],
            dst_ref=sums.at[grp],
            send_sem=send4.at[step],
            recv_sem=recv4.at[grp],
            device_id=place,
            device_id_type=MESH,
        )
        copy.start()
        copies.append(copy)
    for step in range(1, n_grp):
        other, place = sibling(step)
        pltpu.make_async_remote_copy(
            src_ref=sums.at[other],
            dst_ref=sums.at[other],
            send_sem=send4.at[step],
            recv_sem=recv4.at[other],
            device_id=place,
            device_id_type=MESH,
        ).wait_recv()
    total = sums[0]
    for g in range(1, n_grp):
        total = total + sums[g]
    share = row_blocks // n_grp
    result = total[:share]
    for g in range(1, n_grp):
        result = jnp.where(grp == g, total[g * share : (g + 1) * share], result)
    image[...] = result
    for copy in copies:
        copy.wait_send()


def per_device(
    n_slab,
    n_grp,
    echo_data,
    acquirer,
    panels,
    block_count,
    block_rows,
    block_columns,
    apodization,
    window_index,
):
    channels, samples = echo_data.shape[1:]
    n_tx, width, block = panels.shape[1:4]
    n_win = apodization.shape[0]
    n_blocks = samples // block
    row_blocks = window_index.shape[0] // block
    plane = min(4, n_slab, n_blocks // n_grp)
    n_lines = n_slab // plane
    peers = plane * n_grp
    piece = n_blocks // peers
    assert block == LANES and piece * peers == n_blocks and plane * n_lines == n_slab
    unroll = min(16, width)
    dims = (n_grp, plane, n_lines, n_tx, n_win, piece, width, unroll)
    vmem = pl.BlockSpec(memory_space=pltpu.VMEM)
    smem = pl.BlockSpec(memory_space=pltpu.SMEM)
    hbm = pl.BlockSpec(memory_space=pltpu.HBM)
    dma = pltpu.SemaphoreType.DMA
    result = pl.pallas_call(
        functools.partial(kernel, dims),
        out_shape=jax.ShapeDtypeStruct((row_blocks // n_grp, LANES), F32),
        in_specs=[hbm, hbm, vmem, vmem, smem, smem, smem, smem],
        out_specs=vmem,
        scratch_shapes=[
            pltpu.VMEM((peers, channels, piece * LANES), BF16),
            pltpu.VMEM((n_tx, width, block, block), BF16),
            pltpu.VMEM((peers, piece, n_win, LANES), F32),
            pltpu.VMEM((peers, piece, n_win, LANES), F32),
            pltpu.VMEM((n_lines, n_tx, piece, n_win, LANES), F32),
            [pltpu.VMEM((n_blocks, 2 * n_win, LANES), BF16)] * n_tx,
            pltpu.VMEM((row_blocks, n_win, LANES), F32),
            pltpu.VMEM((n_grp, row_blocks, LANES), F32),
            dma((peers,)),
            dma((n_tx,)),
            dma((peers,)),
            dma((peers,)),
            dma((n_tx, n_lines)),
            dma((n_tx, n_lines)),
            dma((n_tx, peers)),
            dma((n_tx, peers)),
            dma((n_grp,)),
            dma((n_grp,)),
        ],
        compiler_params=pltpu.CompilerParams(
            collective_id=0, has_side_effects=True, vmem_limit_bytes=62 * 1024 * 1024
        ),
        name="beamform",
    )(
        echo_data,
        panels,
        apodization,
        window_index.reshape(row_blocks, block),
        acquirer,
        block_count,
        block_rows.transpose(1, 0, 2),
        block_columns.transpose(1, 0, 2),
    )
    return result.reshape(-1)


def solution(mesh):
    return jax.shard_map(
        functools.partial(per_device, mesh.shape["slab"], mesh.shape["grp"]),
        mesh=mesh,
        in_specs=(
            P("slab", "grp", None),
            P(),
            P("slab", None, "grp", None, None),
            P("slab", None),
            P("slab", None, None),
            P("slab", None, None),
            P(None, "grp"),
            P("slab"),
        ),
        out_specs=P(("slab", "grp")),
        check_vma=False,
    )
```

```python
import functools

import jax
import jax.numpy as jnp
from jax import lax
from jax.experimental import pallas as pl
from jax.experimental.pallas import tpu as pltpu
from jax.sharding import PartitionSpec as P

MESH = pl.DeviceIdType.MESH
F32 = jnp.float32
BF16 = jnp.bfloat16
LANES = 128


def split_terms(x, n):
    terms = []
    for _ in range(n):
        term = x.astype(BF16)
        terms.append(term)
        x = x - term.astype(F32)
    return terms


STEPS = 32700.0
FINEST = 16.0


def coded(values):
    lanes = lax.broadcasted_iota(jnp.int32, values[0].shape, 1)
    logs = jnp.zeros(values[0].shape, F32)
    tiles = []
    for number, value in enumerate(values):
        top = jnp.max(jnp.abs(value), axis=1, keepdims=True)
        top = jnp.broadcast_to(jnp.maximum(top, 2.0**-120), value.shape)
        log = jnp.ceil(jnp.log2(top) * FINEST)
        tiles.append(jnp.round(value * jnp.exp2(log * (-1.0 / FINEST)) * STEPS))
        logs = jnp.where(lanes == number, log, logs)
    return tiles, logs


def to_16(x):
    return x.astype(jnp.int32).astype(jnp.int16)


def from_16(x):
    return x.astype(jnp.int32).astype(F32)


def kernel(
    dims,
    echo,
    panels,
    apod,
    windows,
    acquirer,
    counts,
    rows,
    columns,
    image,
    echo_v,
    panels_v,
    own,
    parts,
    line,
    shares,
    tables,
    onehot,
    sums,
    echo_sem,
    panel_sem,
    send1,
    recv1,
    send2,
    recv2,
    send3,
    recv3,
    send4,
    recv4,
):
    n_grp, plane, n_lines, n_tx, n_win, piece, width, unroll = dims
    peers = plane * n_grp
    span = piece * LANES
    slab, grp = lax.axis_index("slab"), lax.axis_index("grp")
    level, spot = slab // plane, slab % plane
    me = spot * n_grp + grp

    def peer(step):
        other = lax.rem(me + step, peers)
        return other, (level * plane + other // n_grp, lax.rem(other, n_grp))

    def along(step):
        other = lax.rem(level + step, n_lines)
        return other, (other * plane + spot, grp)

    def sibling(step):
        other = lax.rem(grp + step, n_grp)
        return other, (slab, other)

    barrier = pltpu.get_barrier_semaphore()
    for step in range(1, peers):
        pl.semaphore_signal(barrier, inc=1, device_id=peer(step)[1], device_id_type=MESH)
    for step in range(1, n_lines):
        pl.semaphore_signal(barrier, inc=1, device_id=along(step)[1], device_id_type=MESH)

    order = [lax.rem(me + step, peers) for step in range(1, peers + 1)]
    loads = []
    for number, part in enumerate(order):
        cut = pl.ds(pl.multiple_of(part * span, span), span)
        load = pltpu.make_async_copy(echo.at[0, :, cut], echo_v.at[number], echo_sem.at[number])
        load.start()
        loads.append(load)
    panel_loads = []
    for t in range(n_tx):
        load = pltpu.make_async_copy(panels.at[0, t], panels_v.at[t], panel_sem.at[t])
        load.start()
        panel_loads.append(load)

    row_blocks = windows.shape[0]
    for r in range(row_blocks):
        ids = lax.broadcasted_iota(jnp.int32, (n_win, LANES), 0)
        onehot[r] = jnp.where(ids == windows[r : r + 1, :], 1.0, 0.0).astype(F32)

    weights = jnp.concatenate(split_terms(apod[...], 3), axis=0)

    pl.semaphore_wait(barrier, peers - 1 + n_lines - 1)

    copies = []
    for number, part in enumerate(order):
        loads[number].wait()
        terms = jnp.dot(weights, echo_v[number], preferred_element_type=F32)
        value = terms[:n_win] + terms[n_win : 2 * n_win] + terms[2 * n_win :]
        for c in range(piece):
            chunk = value[:, c * LANES : (c + 1) * LANES]
            if number == peers - 1:
                parts[me, c] = chunk
            else:
                own[number, c] = chunk
        if number < peers - 1:
            copy = pltpu.make_async_remote_copy(
                src_ref=own.at[number],
                dst_ref=parts.at[me],
                send_sem=send1.at[number],
                recv_sem=recv1.at[me],
                device_id=peer(number + 1)[1],
                device_id_type=MESH,
            )
            copy.start()
            copies.append(copy)
    for step in range(1, peers):
        other, place = peer(step)
        pltpu.make_async_remote_copy(
            src_ref=own.at[0],
            dst_ref=parts.at[other],
            send_sem=send1.at[0],
            recv_sem=recv1.at[other],
            device_id=place,
            device_id_type=MESH,
        ).wait_recv()

    records = []
    for c in range(piece):
        for q in range(plane):
            total = parts[q * n_grp, c]
            for g in range(1, n_grp):
                total = total + parts[q * n_grp + g, c]
            records.append(total)
    values = []
    held = []
    for t in range(n_tx):
        holder = jnp.full((n_win, LANES), acquirer[t], jnp.int32) - level * plane
        held.append((holder >= 0) & (holder < plane))
        for c in range(piece):
            value = jnp.zeros((n_win, LANES), F32)
            for q in range(plane):
                value = jnp.where(holder == q, records[c * plane + q], value)
            values.append(value)
    tiles, logs = coded(values)
    lanes = lax.broadcasted_iota(jnp.int32, (n_win, LANES), 1)
    kept = jnp.zeros((n_win, LANES), F32)
    for t in range(n_tx):
        inside = (lanes >= t * piece) & (lanes < (t + 1) * piece)
        kept = kept + jnp.where(inside & held[t], logs, 0.0)
    line[level, 0] = to_16(kept)

    def span_of(t):
        return pl.ds(0, piece + 1) if t == 0 else pl.ds(1 + t * piece, piece)

    for t in range(n_tx):
        for c in range(piece):
            line[level, 1 + t * piece + c] = to_16(tiles[t * piece + c])
        for step in range(1, n_lines):
            other, place = along(step)
            copy = pltpu.make_async_remote_copy(
                src_ref=line.at[level, span_of(t)],
                dst_ref=line.at[level, span_of(t)],
                send_sem=send2.at[t, step],
                recv_sem=recv2.at[t, level],
                device_id=place,
                device_id_type=MESH,
            )
            copy.start()
            copies.append(copy)

    for t in range(n_tx):
        for step in range(1, n_lines):
            other, place = along(step)
            pltpu.make_async_remote_copy(
                src_ref=line.at[other, span_of(t)],
                dst_ref=line.at[other, span_of(t)],
                send_sem=send2.at[t, step],
                recv_sem=recv2.at[t, other],
                device_id=place,
                device_id_type=MESH,
            ).wait_recv()
        first = 0 if t == 0 else 1 + t * piece
        for c in range(shares[t].shape[1]):
            value = line[0, first + c].astype(jnp.int32)
            for l in range(1, n_lines):
                value = value + line[l, first + c].astype(jnp.int32)
            shares[t][me, c] = value.astype(jnp.int16)
        for step in range(1, peers):
            other, place = peer(step)
            copy = pltpu.make_async_remote_copy(
                src_ref=shares[t].at[me],
                dst_ref=shares[t].at[me],
                send_sem=send3.at[t, step],
                recv_sem=recv3.at[t, me],
                device_id=place,
                device_id_type=MESH,
            )
            copy.start()
            copies.append(copy)

    row_ids = lax.broadcasted_iota(jnp.int32, (row_blocks, LANES), 0)
    acc = jnp.zeros((row_blocks, LANES), F32)
    for t in range(n_tx):
        panel_loads[t].wait()
        for step in range(1, peers):
            other, place = peer(step)
            pltpu.make_async_remote_copy(
                src_ref=shares[t].at[other],
                dst_ref=shares[t].at[other],
                send_sem=send3.at[t, step],
                recv_sem=recv3.at[t, other],
                device_id=place,
                device_id_type=MESH,
            ).wait_recv()
        if t == 0:
            scales = [
                jnp.exp2(from_16(shares[0][p, 0]) * (1.0 / FINEST)) * (1.0 / STEPS)
                for p in range(peers)
            ]
        for p in range(peers):
            for c in range(piece):
                lane = t * piece + c
                value = from_16(shares[t][p, c + (t == 0)]) * scales[p][:, lane : lane + 1]
                tables[t][p * piece + c] = jnp.concatenate(split_terms(value, 2), axis=0)

        def some_slots(turn, acc, t=t):
            for u in range(unroll):
                k = turn * unroll + u
                slot = grp * width + k
                r = rows[t, 0, slot]
                signal = tables[t][columns[t, 0, slot]]
                both = lax.dot_general(
                    signal,
                    panels_v[t, k],
                    (((1,), (1,)), ((), ())),
                    preferred_element_type=F32,
                )
                value = (both[:n_win] + both[n_win:]) * onehot[r]
                value = jnp.sum(value, axis=0, keepdims=True)
                target = jnp.where(slot < counts[0, t], r, -1)
                acc = acc + jnp.where(row_ids == target, value, 0.0)
            return acc

        acc = lax.fori_loop(0, width // unroll, some_slots, acc)

    sums[grp] = acc
    for step in range(1, n_grp):
        other, place = sibling(step)
        copy = pltpu.make_async_remote_copy(
            src_ref=sums.at[grp],
            dst_ref=sums.at[grp],
            send_sem=send4.at[step],
            recv_sem=recv4.at[grp],
            device_id=place,
            device_id_type=MESH,
        )
        copy.start()
        copies.append(copy)
    for step in range(1, n_grp):
        other, place = sibling(step)
        pltpu.make_async_remote_copy(
            src_ref=sums.at[other],
            dst_ref=sums.at[other],
            send_sem=send4.at[step],
            recv_sem=recv4.at[other],
            device_id=place,
            device_id_type=MESH,
        ).wait_recv()
    total = sums[0]
    for g in range(1, n_grp):
        total = total + sums[g]
    share = row_blocks // n_grp
    result = total[:share]
    for g in range(1, n_grp):
        result = jnp.where(grp == g, total[g * share : (g + 1) * share], result)
    image[...] = result
    for copy in copies:
        copy.wait_send()


def per_device(
    n_slab,
    n_grp,
    echo_data,
    acquirer,
    panels,
    block_count,
    block_rows,
    block_columns,
    apodization,
    window_index,
):
    channels, samples = echo_data.shape[1:]
    n_tx, width, block = panels.shape[1:4]
    n_win = apodization.shape[0]
    n_blocks = samples // block
    row_blocks = window_index.shape[0] // block
    plane = min(4, n_slab, n_blocks // n_grp)
    n_lines = n_slab // plane
    peers = plane * n_grp
    piece = n_blocks // peers
    assert block == LANES and piece * peers == n_blocks and plane * n_lines == n_slab
    unroll = min(16, width)
    dims = (n_grp, plane, n_lines, n_tx, n_win, piece, width, unroll)
    vmem = pl.BlockSpec(memory_space=pltpu.VMEM)
    smem = pl.BlockSpec(memory_space=pltpu.SMEM)
    hbm = pl.BlockSpec(memory_space=pltpu.HBM)
    dma = pltpu.SemaphoreType.DMA
    result = pl.pallas_call(
        functools.partial(kernel, dims),
        out_shape=jax.ShapeDtypeStruct((row_blocks // n_grp, LANES), F32),
        in_specs=[hbm, hbm, vmem, vmem, smem, smem, smem, smem],
        out_specs=vmem,
        scratch_shapes=[
            pltpu.VMEM((peers, channels, piece * LANES), BF16),
            pltpu.VMEM((n_tx, width, block, block), BF16),
            pltpu.VMEM((peers, piece, n_win, LANES), F32),
            pltpu.VMEM((peers, piece, n_win, LANES), F32),
            pltpu.VMEM((n_lines, n_tx * piece + 1, n_win, LANES), jnp.int16),
            [
                pltpu.VMEM((peers, piece + (t == 0), n_win, LANES), jnp.int16)
                for t in range(n_tx)
            ],
            [pltpu.VMEM((n_blocks, 2 * n_win, LANES), BF16)] * n_tx,
            pltpu.VMEM((row_blocks, n_win, LANES), F32),
            pltpu.VMEM((n_grp, row_blocks, LANES), F32),
            dma((peers,)),
            dma((n_tx,)),
            dma((peers,)),
            dma((peers,)),
            dma((n_tx, n_lines)),
            dma((n_tx, n_lines)),
            dma((n_tx, peers)),
            dma((n_tx, peers)),
            dma((n_grp,)),
            dma((n_grp,)),
        ],
        compiler_params=pltpu.CompilerParams(
            collective_id=0, has_side_effects=True, vmem_limit_bytes=62 * 1024 * 1024
        ),
        name="beamform",
    )(
        echo_data,
        panels,
        apodization,
        window_index.reshape(row_blocks, block),
        acquirer,
        block_count,
        block_rows.transpose(1, 0, 2),
        block_columns.transpose(1, 0, 2),
    )
    return result.reshape(-1)


def solution(mesh):
    return jax.shard_map(
        functools.partial(per_device, mesh.shape["slab"], mesh.shape["grp"]),
        mesh=mesh,
        in_specs=(
            P("slab", "grp", None),
            P(),
            P("slab", None, "grp", None, None),
            P("slab", None),
            P("slab", None, None),
            P("slab", None, None),
            P(None, "grp"),
            P("slab"),
        ),
        out_specs=P(("slab", "grp")),
        check_vma=False,
    )
```

```python
import functools

import jax
import jax.numpy as jnp
from jax import lax
from jax.experimental import pallas as pl
from jax.experimental.pallas import tpu as pltpu
from jax.sharding import PartitionSpec as P

MESH = pl.DeviceIdType.MESH
F32 = jnp.float32
BF16 = jnp.bfloat16
LANES = 128


def split_terms(x, n):
    terms = []
    for _ in range(n):
        term = x.astype(BF16)
        terms.append(term)
        x = x - term.astype(F32)
    return terms


def kernel(
    dims,
    echo,
    panels,
    apod,
    windows,
    acquirer,
    counts,
    rows,
    columns,
    image,
    echo_v,
    panels_v,
    own,
    parts,
    line,
    tables,
    onehot,
    sums,
    echo_sem,
    panel_sem,
    send1,
    recv1,
    send2,
    recv2,
    send3,
    recv3,
    send4,
    recv4,
):
    n_grp, plane, n_lines, n_tx, n_win, piece, width, unroll = dims
    peers = plane * n_grp
    span = piece * LANES
    slab, grp = lax.axis_index("slab"), lax.axis_index("grp")
    level, spot = slab // plane, slab % plane
    me = spot * n_grp + grp

    def peer(step):
        other = lax.rem(me + step, peers)
        return other, (level * plane + other // n_grp, lax.rem(other, n_grp))

    def along(step):
        other = lax.rem(level + step, n_lines)
        return other, (other * plane + spot, grp)

    def sibling(step):
        other = lax.rem(grp + step, n_grp)
        return other, (slab, other)

    barrier = pltpu.get_barrier_semaphore()
    for step in range(1, peers):
        pl.semaphore_signal(barrier, inc=1, device_id=peer(step)[1], device_id_type=MESH)
    for step in range(1, n_lines):
        pl.semaphore_signal(barrier, inc=1, device_id=along(step)[1], device_id_type=MESH)

    order = [lax.rem(me + step, peers) for step in range(1, peers + 1)]
    loads = []
    for number, part in enumerate(order):
        cut = pl.ds(pl.multiple_of(part * span, span), span)
        load = pltpu.make_async_copy(echo.at[0, :, cut], echo_v.at[number], echo_sem.at[number])
        load.start()
        loads.append(load)
    panel_loads = []
    for t in range(n_tx):
        load = pltpu.make_async_copy(panels.at[0, t], panels_v.at[t], panel_sem.at[t])
        panel_loads.append(load)

    row_blocks = windows.shape[0]
    for r in range(row_blocks):
        ids = lax.broadcasted_iota(jnp.int32, (n_win, LANES), 0)
        onehot[r] = jnp.where(ids == windows[r : r + 1, :], 1.0, 0.0).astype(F32)

    weights = jnp.concatenate(split_terms(apod[...], 3), axis=0)

    pl.semaphore_wait(barrier, peers - 1 + n_lines - 1)

    copies = []
    half = peers // 2
    for group in (range(half), range(half, peers)):
        for number in group:
            loads[number].wait()
        if group[-1] == peers - 1:
            for load in panel_loads:
                load.start()
        for number in group:
            terms = jnp.dot(weights, echo_v[number], preferred_element_type=F32)
            value = terms[:n_win] + terms[n_win : 2 * n_win] + terms[2 * n_win :]
            for c in range(piece):
                chunk = value[:, c * LANES : (c + 1) * LANES]
                if number == peers - 1:
                    parts[me, c] = chunk
                else:
                    own[number, c] = chunk
        for number in group:
            if number < peers - 1:
                copy = pltpu.make_async_remote_copy(
                    src_ref=own.at[number],
                    dst_ref=parts.at[me],
                    send_sem=send1.at[number],
                    recv_sem=recv1.at[me],
                    device_id=peer(number + 1)[1],
                    device_id_type=MESH,
                )
                copy.start()
                copies.append(copy)
    for step in range(1, peers):
        other, place = peer(step)
        pltpu.make_async_remote_copy(
            src_ref=own.at[0],
            dst_ref=parts.at[other],
            send_sem=send1.at[0],
            recv_sem=recv1.at[other],
            device_id=place,
            device_id_type=MESH,
        ).wait_recv()

    records = []
    for c in range(piece):
        for q in range(plane):
            total = parts[q * n_grp, c]
            for g in range(1, n_grp):
                total = total + parts[q * n_grp + g, c]
            records.append(total)
    for t in range(n_tx):
        for c in range(piece):
            value = jnp.zeros((n_win, LANES), F32)
            for q in range(plane):
                hit = jnp.full((n_win, LANES), acquirer[t], jnp.int32) == level * plane + q
                value = value + jnp.where(hit, records[c * plane + q], 0.0)
            line[level, t, c] = value
        for step in range(1, n_lines):
            other, place = along(step)
            copy = pltpu.make_async_remote_copy(
                src_ref=line.at[level, t],
                dst_ref=line.at[level, t],
                send_sem=send2.at[t, step],
                recv_sem=recv2.at[t, level],
                device_id=place,
                device_id_type=MESH,
            )
            copy.start()
            copies.append(copy)

    mine = pl.ds(me * piece, piece)
    for t in range(n_tx):
        for step in range(1, n_lines):
            other, place = along(step)
            pltpu.make_async_remote_copy(
                src_ref=line.at[other, t],
                dst_ref=line.at[other, t],
                send_sem=send2.at[t, step],
                recv_sem=recv2.at[t, other],
                device_id=place,
                device_id_type=MESH,
            ).wait_recv()
        for c in range(piece):
            value = line[0, t, c]
            for l in range(1, n_lines):
                value = value + line[l, t, c]
            tables[t][me * piece + c] = jnp.concatenate(split_terms(value, 2), axis=0)
        for step in range(1, peers):
            other, place = peer(step)
            copy = pltpu.make_async_remote_copy(
                src_ref=tables[t].at[mine],
                dst_ref=tables[t].at[mine],
                send_sem=send3.at[t, step],
                recv_sem=recv3.at[t, me],
                device_id=place,
                device_id_type=MESH,
            )
            copy.start()
            copies.append(copy)

    row_ids = lax.broadcasted_iota(jnp.int32, (row_blocks, LANES), 0)
    acc = jnp.zeros((row_blocks, LANES), F32)
    for t in range(n_tx):
        panel_loads[t].wait()
        for step in range(1, peers):
            other, place = peer(step)
            theirs = pl.ds(other * piece, piece)
            pltpu.make_async_remote_copy(
                src_ref=tables[t].at[theirs],
                dst_ref=tables[t].at[theirs],
                send_sem=send3.at[t, step],
                recv_sem=recv3.at[t, other],
                device_id=place,
                device_id_type=MESH,
            ).wait_recv()

        def some_slots(turn, acc, t=t):
            for pair in range(unroll // 2):
                first = turn * unroll + 2 * pair
                signals = [
                    tables[t][columns[t, 0, grp * width + first + i]] for i in range(2)
                ]
                both = lax.dot_general(
                    jnp.concatenate(signals, axis=0),
                    panels_v[t, pl.ds(first, 2)].reshape(2 * LANES, LANES),
                    (((1,), (1,)), ((), ())),
                    preferred_element_type=F32,
                )
                for i in range(2):
                    slot = grp * width + first + i
                    r = rows[t, 0, slot]
                    own_part = both[2 * n_win * i :, i * LANES : (i + 1) * LANES]
                    value = (own_part[:n_win] + own_part[n_win : 2 * n_win]) * onehot[r]
                    value = jnp.sum(value, axis=0, keepdims=True)
                    target = jnp.where(slot < counts[0, t], r, -1)
                    acc = acc + jnp.where(row_ids == target, value, 0.0)
            return acc

        acc = lax.fori_loop(0, width // unroll, some_slots, acc)

    sums[grp] = acc
    for step in range(1, n_grp):
        other, place = sibling(step)
        copy = pltpu.make_async_remote_copy(
            src_ref=sums.at[grp],
            dst_ref=sums.at[grp],
            send_sem=send4.at[step],
            recv_sem=recv4.at[grp],
            device_id=place,
            device_id_type=MESH,
        )
        copy.start()
        copies.append(copy)
    for step in range(1, n_grp):
        other, place = sibling(step)
        pltpu.make_async_remote_copy(
            src_ref=sums.at[other],
            dst_ref=sums.at[other],
            send_sem=send4.at[step],
            recv_sem=recv4.at[other],
            device_id=place,
            device_id_type=MESH,
        ).wait_recv()
    total = sums[0]
    for g in range(1, n_grp):
        total = total + sums[g]
    share = row_blocks // n_grp
    result = total[:share]
    for g in range(1, n_grp):
        result = jnp.where(grp == g, total[g * share : (g + 1) * share], result)
    image[...] = result
    for copy in copies:
        copy.wait_send()


def per_device(
    n_slab,
    n_grp,
    echo_data,
    acquirer,
    panels,
    block_count,
    block_rows,
    block_columns,
    apodization,
    window_index,
):
    channels, samples = echo_data.shape[1:]
    n_tx, width, block = panels.shape[1:4]
    n_win = apodization.shape[0]
    n_blocks = samples // block
    row_blocks = window_index.shape[0] // block
    plane = min(4, n_slab, n_blocks // n_grp)
    n_lines = n_slab // plane
    peers = plane * n_grp
    piece = n_blocks // peers
    assert block == LANES and piece * peers == n_blocks and plane * n_lines == n_slab
    unroll = min(16, width)
    dims = (n_grp, plane, n_lines, n_tx, n_win, piece, width, unroll)
    vmem = pl.BlockSpec(memory_space=pltpu.VMEM)
    smem = pl.BlockSpec(memory_space=pltpu.SMEM)
    hbm = pl.BlockSpec(memory_space=pltpu.HBM)
    dma = pltpu.SemaphoreType.DMA
    result = pl.pallas_call(
        functools.partial(kernel, dims),
        out_shape=jax.ShapeDtypeStruct((row_blocks // n_grp, LANES), F32),
        in_specs=[hbm, hbm, vmem, vmem, smem, smem, smem, smem],
        out_specs=vmem,
        scratch_shapes=[
            pltpu.VMEM((peers, channels, piece * LANES), BF16),
            pltpu.VMEM((n_tx, width, block, block), BF16),
            pltpu.VMEM((peers, piece, n_win, LANES), F32),
            pltpu.VMEM((peers, piece, n_win, LANES), F32),
            pltpu.VMEM((n_lines, n_tx, piece, n_win, LANES), F32),
            [pltpu.VMEM((n_blocks, 2 * n_win, LANES), BF16)] * n_tx,
            pltpu.VMEM((row_blocks, n_win, LANES), F32),
            pltpu.VMEM((n_grp, row_blocks, LANES), F32),
            dma((peers,)),
            dma((n_tx,)),
            dma((peers,)),
            dma((peers,)),
            dma((n_tx, n_lines)),
            dma((n_tx, n_lines)),
            dma((n_tx, peers)),
            dma((n_tx, peers)),
            dma((n_grp,)),
            dma((n_grp,)),
        ],
        compiler_params=pltpu.CompilerParams(
            collective_id=0, has_side_effects=True, vmem_limit_bytes=62 * 1024 * 1024
        ),
        name="beamform",
    )(
        echo_data,
        panels,
        apodization,
        window_index.reshape(row_blocks, block),
        acquirer,
        block_count,
        block_rows.transpose(1, 0, 2),
        block_columns.transpose(1, 0, 2),
    )
    return result.reshape(-1)


def solution(mesh):
    return jax.shard_map(
        functools.partial(per_device, mesh.shape["slab"], mesh.shape["grp"]),
        mesh=mesh,
        in_specs=(
            P("slab", "grp", None),
            P(),
            P("slab", None, "grp", None, None),
            P("slab", None),
            P("slab", None, None),
            P("slab", None, None),
            P(None, "grp"),
            P("slab"),
        ),
        out_specs=P(("slab", "grp")),
        check_vma=False,
    )
```

```python
import functools

import jax
import jax.numpy as jnp
from jax import lax
from jax.experimental import pallas as pl
from jax.experimental.pallas import tpu as pltpu
from jax.sharding import PartitionSpec as P

MESH = pl.DeviceIdType.MESH
F32 = jnp.float32
BF16 = jnp.bfloat16
LANES = 128


def split_terms(x, n):
    terms = []
    for _ in range(n):
        term = x.astype(BF16)
        terms.append(term)
        x = x - term.astype(F32)
    return terms


def kernel(
    dims,
    echo,
    panels,
    apod_in,
    windows_in,
    acquirer_in,
    counts_in,
    rows_in,
    columns_in,
    image,
    apod,
    windows,
    acquirer,
    counts,
    rows,
    columns,
    small_sem,
    echo_v,
    panels_v,
    own,
    parts,
    line,
    tables,
    onehot,
    sums,
    echo_sem,
    panel_sem,
    send1,
    recv1,
    send2,
    recv2,
    send3,
    recv3,
    send4,
    recv4,
):
    n_grp, plane, n_lines, n_tx, n_win, piece, width, unroll = dims
    peers = plane * n_grp
    span = piece * LANES
    slab, grp = lax.axis_index("slab"), lax.axis_index("grp")
    level, spot = slab // plane, slab % plane
    me = spot * n_grp + grp

    def peer(step):
        other = lax.rem(me + step, peers)
        return other, (level * plane + other // n_grp, lax.rem(other, n_grp))

    def along(step):
        other = lax.rem(level + step, n_lines)
        return other, (other * plane + spot, grp)

    def sibling(step):
        other = lax.rem(grp + step, n_grp)
        return other, (slab, other)

    barrier = pltpu.get_barrier_semaphore()
    for step in range(1, peers):
        pl.semaphore_signal(barrier, inc=1, device_id=peer(step)[1], device_id_type=MESH)
    for step in range(1, n_lines):
        pl.semaphore_signal(barrier, inc=1, device_id=along(step)[1], device_id_type=MESH)

    small = [
        pltpu.make_async_copy(source, target, small_sem.at[number])
        for number, (source, target) in enumerate(
            (
                (apod_in, apod),
                (acquirer_in, acquirer),
                (windows_in, windows),
                (counts_in, counts),
                (rows_in, rows),
                (columns_in, columns),
            )
        )
    ]
    small[0].start()
    order = [lax.rem(me + step, peers) for step in range(1, peers + 1)]
    loads = []
    for number, part in enumerate(order):
        cut = pl.ds(pl.multiple_of(part * span, span), span)
        load = pltpu.make_async_copy(echo.at[0, :, cut], echo_v.at[number], echo_sem.at[number])
        load.start()
        loads.append(load)
    panel_loads = []
    for t in range(n_tx):
        load = pltpu.make_async_copy(panels.at[0, t], panels_v.at[t], panel_sem.at[t])
        panel_loads.append(load)

    for load in small[1:]:
        load.start()

    small[0].wait()
    weights = jnp.concatenate(split_terms(apod[...], 3), axis=0)

    pl.semaphore_wait(barrier, peers - 1 + n_lines - 1)

    copies = []
    half = peers // 2
    for group in (range(half), range(half, peers)):
        for number in group:
            loads[number].wait()
        if group[-1] == peers - 1:
            for load in panel_loads:
                load.start()
        for number in group:
            terms = jnp.dot(weights, echo_v[number], preferred_element_type=F32)
            value = terms[:n_win] + terms[n_win : 2 * n_win] + terms[2 * n_win :]
            for c in range(piece):
                chunk = value[:, c * LANES : (c + 1) * LANES]
                if number == peers - 1:
                    parts[me, c] = chunk
                else:
                    own[number, c] = chunk
        for number in group:
            if number < peers - 1:
                copy = pltpu.make_async_remote_copy(
                    src_ref=own.at[number],
                    dst_ref=parts.at[me],
                    send_sem=send1.at[number],
                    recv_sem=recv1.at[me],
                    device_id=peer(number + 1)[1],
                    device_id_type=MESH,
                )
                copy.start()
                copies.append(copy)
    for load in small[1:]:
        load.wait()
    row_blocks = windows.shape[0]
    for r in range(row_blocks):
        ids = lax.broadcasted_iota(jnp.int32, (n_win, LANES), 0)
        onehot[r] = jnp.where(ids == windows[r : r + 1, :], 1.0, 0.0).astype(F32)

    for step in range(1, peers):
        other, place = peer(step)
        pltpu.make_async_remote_copy(
            src_ref=own.at[0],
            dst_ref=parts.at[other],
            send_sem=send1.at[0],
            recv_sem=recv1.at[other],
            device_id=place,
            device_id_type=MESH,
        ).wait_recv()

    records = []
    for c in range(piece):
        for q in range(plane):
            total = parts[q * n_grp, c]
            for g in range(1, n_grp):
                total = total + parts[q * n_grp + g, c]
            records.append(total)
    for t in range(n_tx):
        for c in range(piece):
            value = jnp.zeros((n_win, LANES), F32)
            for q in range(plane):
                hit = jnp.full((n_win, LANES), acquirer[t], jnp.int32) == level * plane + q
                value = value + jnp.where(hit, records[c * plane + q], 0.0)
            line[level, t, c] = value
        for step in range(1, n_lines):
            other, place = along(step)
            copy = pltpu.make_async_remote_copy(
                src_ref=line.at[level, t],
                dst_ref=line.at[level, t],
                send_sem=send2.at[t, step],
                recv_sem=recv2.at[t, level],
                device_id=place,
                device_id_type=MESH,
            )
            copy.start()
            copies.append(copy)

    mine = pl.ds(me * piece, piece)
    for t in range(n_tx):
        for step in range(1, n_lines):
            other, place = along(step)
            pltpu.make_async_remote_copy(
                src_ref=line.at[other, t],
                dst_ref=line.at[other, t],
                send_sem=send2.at[t, step],
                recv_sem=recv2.at[t, other],
                device_id=place,
                device_id_type=MESH,
            ).wait_recv()
        for c in range(piece):
            value = line[0, t, c]
            for l in range(1, n_lines):
                value = value + line[l, t, c]
            tables[t][me * piece + c] = jnp.concatenate(split_terms(value, 2), axis=0)
        for step in range(1, peers):
            other, place = peer(step)
            copy = pltpu.make_async_remote_copy(
                src_ref=tables[t].at[mine],
                dst_ref=tables[t].at[mine],
                send_sem=send3.at[t, step],
                recv_sem=recv3.at[t, me],
                device_id=place,
                device_id_type=MESH,
            )
            copy.start()
            copies.append(copy)

    row_ids = lax.broadcasted_iota(jnp.int32, (row_blocks, LANES), 0)
    acc = jnp.zeros((row_blocks, LANES), F32)
    for t in range(n_tx):
        panel_loads[t].wait()
        for step in range(1, peers):
            other, place = peer(step)
            theirs = pl.ds(other * piece, piece)
            pltpu.make_async_remote_copy(
                src_ref=tables[t].at[theirs],
                dst_ref=tables[t].at[theirs],
                send_sem=send3.at[t, step],
                recv_sem=recv3.at[t, other],
                device_id=place,
                device_id_type=MESH,
            ).wait_recv()

        def some_slots(turn, acc, t=t):
            for pair in range(unroll // 2):
                first = turn * unroll + 2 * pair
                signals = [
                    tables[t][columns[t, 0, grp * width + first + i]] for i in range(2)
                ]
                both = lax.dot_general(
                    jnp.concatenate(signals, axis=0),
                    panels_v[t, pl.ds(first, 2)].reshape(2 * LANES, LANES),
                    (((1,), (1,)), ((), ())),
                    preferred_element_type=F32,
                )
                for i in range(2):
                    slot = grp * width + first + i
                    r = rows[t, 0, slot]
                    own_part = both[2 * n_win * i :, i * LANES : (i + 1) * LANES]
                    value = (own_part[:n_win] + own_part[n_win : 2 * n_win]) * onehot[r]
                    value = jnp.sum(value, axis=0, keepdims=True)
                    target = jnp.where(slot < counts[0, t], r, -1)
                    acc = acc + jnp.where(row_ids == target, value, 0.0)
            return acc

        acc = lax.fori_loop(0, width // unroll, some_slots, acc)

    sums[grp] = acc
    for step in range(1, n_grp):
        other, place = sibling(step)
        copy = pltpu.make_async_remote_copy(
            src_ref=sums.at[grp],
            dst_ref=sums.at[grp],
            send_sem=send4.at[step],
            recv_sem=recv4.at[grp],
            device_id=place,
            device_id_type=MESH,
        )
        copy.start()
        copies.append(copy)
    for step in range(1, n_grp):
        other, place = sibling(step)
        pltpu.make_async_remote_copy(
            src_ref=sums.at[other],
            dst_ref=sums.at[other],
            send_sem=send4.at[step],
            recv_sem=recv4.at[other],
            device_id=place,
            device_id_type=MESH,
        ).wait_recv()
    total = sums[0]
    for g in range(1, n_grp):
        total = total + sums[g]
    share = row_blocks // n_grp
    result = total[:share]
    for g in range(1, n_grp):
        result = jnp.where(grp == g, total[g * share : (g + 1) * share], result)
    image[...] = result
    for copy in copies:
        copy.wait_send()


def per_device(
    n_slab,
    n_grp,
    echo_data,
    acquirer,
    panels,
    block_count,
    block_rows,
    block_columns,
    apodization,
    window_index,
):
    channels, samples = echo_data.shape[1:]
    n_tx, width, block = panels.shape[1:4]
    n_win = apodization.shape[0]
    n_blocks = samples // block
    row_blocks = window_index.shape[0] // block
    plane = min(4, n_slab, n_blocks // n_grp)
    n_lines = n_slab // plane
    peers = plane * n_grp
    piece = n_blocks // peers
    assert block == LANES and piece * peers == n_blocks and plane * n_lines == n_slab
    unroll = min(16, width)
    dims = (n_grp, plane, n_lines, n_tx, n_win, piece, width, unroll)
    vmem = pl.BlockSpec(memory_space=pltpu.VMEM)
    hbm = pl.BlockSpec(memory_space=pltpu.HBM)
    dma = pltpu.SemaphoreType.DMA
    result = pl.pallas_call(
        functools.partial(kernel, dims),
        out_shape=jax.ShapeDtypeStruct((row_blocks // n_grp, LANES), F32),
        in_specs=[hbm] * 8,
        out_specs=vmem,
        scratch_shapes=[
            pltpu.VMEM(apodization.shape, F32),
            pltpu.VMEM((row_blocks, block), jnp.int32),
            pltpu.SMEM(acquirer.shape, jnp.int32),
            pltpu.SMEM(block_count.shape, jnp.int32),
            pltpu.SMEM((n_tx, 1, block_rows.shape[2]), jnp.int32),
            pltpu.SMEM((n_tx, 1, block_columns.shape[2]), jnp.int32),
            dma((6,)),
            pltpu.VMEM((peers, channels, piece * LANES), BF16),
            pltpu.VMEM((n_tx, width, block, block), BF16),
            pltpu.VMEM((peers, piece, n_win, LANES), F32),
            pltpu.VMEM((peers, piece, n_win, LANES), F32),
            pltpu.VMEM((n_lines, n_tx, piece, n_win, LANES), F32),
            [pltpu.VMEM((n_blocks, 2 * n_win, LANES), BF16)] * n_tx,
            pltpu.VMEM((row_blocks, n_win, LANES), F32),
            pltpu.VMEM((n_grp, row_blocks, LANES), F32),
            dma((peers,)),
            dma((n_tx,)),
            dma((peers,)),
            dma((peers,)),
            dma((n_tx, n_lines)),
            dma((n_tx, n_lines)),
            dma((n_tx, peers)),
            dma((n_tx, peers)),
            dma((n_grp,)),
            dma((n_grp,)),
        ],
        compiler_params=pltpu.CompilerParams(
            collective_id=0, has_side_effects=True, vmem_limit_bytes=62 * 1024 * 1024
        ),
        name="beamform",
    )(
        echo_data,
        panels,
        apodization,
        window_index.reshape(row_blocks, block),
        acquirer,
        block_count,
        block_rows.transpose(1, 0, 2),
        block_columns.transpose(1, 0, 2),
    )
    return result.reshape(-1)


def solution(mesh):
    return jax.shard_map(
        functools.partial(per_device, mesh.shape["slab"], mesh.shape["grp"]),
        mesh=mesh,
        in_specs=(
            P("slab", "grp", None),
            P(),
            P("slab", None, "grp", None, None),
            P("slab", None),
            P("slab", None, None),
            P("slab", None, None),
            P(None, "grp"),
            P("slab"),
        ),
        out_specs=P(("slab", "grp")),
        check_vma=False,
    )
```

```python
import functools
import math

import jax
import jax.numpy as jnp
from jax import lax
from jax.experimental import pallas as pl
from jax.experimental.pallas import tpu as pltpu
from jax.sharding import PartitionSpec as P

MESH = pl.DeviceIdType.MESH
F32 = jnp.float32
BF16 = jnp.bfloat16
LANES = 128


def split_terms(x, n):
    terms = []
    for _ in range(n):
        term = x.astype(BF16)
        terms.append(term)
        x = x - term.astype(F32)
    return terms


def each(low, high, step):
    def body(i, carry):
        step(i)
        return carry

    lax.fori_loop(low, high, body, 0)


def kernel(
    dims,
    echo,
    panels,
    apod_in,
    windows_in,
    acquirer_in,
    counts_in,
    rows_in,
    columns_in,
    image,
    apod,
    windows,
    acquirer,
    counts,
    rows,
    columns,
    small_sem,
    echo_v,
    panels_v,
    own,
    parts,
    line,
    tables,
    onehot,
    sums,
    echo_sem,
    panel_sem,
    send1,
    recv1,
    send2,
    recv2,
    send3,
    recv3,
    send4,
    recv4,
):
    n_grp, plane, n_lines, n_tx, n_win, piece, width, unroll = dims
    peers = plane * n_grp
    span = piece * LANES
    slab, grp = lax.axis_index("slab"), lax.axis_index("grp")
    level, spot = slab // plane, slab % plane
    me = spot * n_grp + grp

    def peer(step):
        other = lax.rem(me + step, peers)
        return other, (level * plane + other // n_grp, lax.rem(other, n_grp))

    def along(step):
        other = lax.rem(level + step, n_lines)
        return other, (other * plane + spot, grp)

    def sibling(step):
        other = lax.rem(grp + step, n_grp)
        return other, (slab, other)

    barrier = pltpu.get_barrier_semaphore()

    def greet(place):
        pl.semaphore_signal(barrier, inc=1, device_id=place, device_id_type=MESH)

    each(1, peers, lambda step: greet(peer(step)[1]))
    each(1, n_lines, lambda step: greet(along(step)[1]))

    small = [
        pltpu.make_async_copy(source, target, small_sem.at[number])
        for number, (source, target) in enumerate(
            (
                (apod_in, apod),
                (acquirer_in, acquirer),
                (windows_in, windows),
                (counts_in, counts),
                (rows_in, rows),
                (columns_in, columns),
            )
        )
    ]
    small[0].start()
    turns = math.gcd(peers, 4)
    chunks = peers // turns

    def record_load(number):
        part = lax.rem(me + number + 1, peers)
        cut = pl.ds(pl.multiple_of(part * span, span), span)
        return pltpu.make_async_copy(
            echo.at[0, :, cut], echo_v.at[number], echo_sem.at[number]
        )

    def send_load(number):
        record_load(number).start()

    each(0, peers, send_load)
    panel_loads = [
        pltpu.make_async_copy(panels.at[0, t], panels_v.at[t], panel_sem.at[t])
        for t in range(n_tx)
    ]

    for load in small[1:]:
        load.start()

    small[0].wait()
    weights = jnp.concatenate(split_terms(apod[...], 3), axis=0)

    pl.semaphore_wait(barrier, peers - 1 + n_lines - 1)

    def send_piece(step):
        other, place = peer(step)
        return pltpu.make_async_remote_copy(
            src_ref=own.at[step - 1],
            dst_ref=parts.at[me],
            send_sem=send1.at[step - 1],
            recv_sem=recv1.at[me],
            device_id=place,
            device_id_type=MESH,
        )

    def some_chunks(turn):
        for u in range(chunks):
            record_load(turn * chunks + u).wait()
        for u in range(chunks):
            number = turn * chunks + u
            terms = jnp.dot(weights, echo_v[number], preferred_element_type=F32)
            value = terms[:n_win] + terms[n_win : 2 * n_win] + terms[2 * n_win :]
            for c in range(piece):
                own[number, c] = value[:, c * LANES : (c + 1) * LANES]
        for u in range(chunks):
            number = turn * chunks + u

            @pl.when(number < peers - 1)
            def _():
                send_piece(number + 1).start()

    each(0, turns, some_chunks)
    parts[me] = own[peers - 1]
    for load in panel_loads:
        load.start()
    copies = []
    for load in small[1:]:
        load.wait()
    row_blocks = windows.shape[0]
    for r in range(row_blocks):
        ids = lax.broadcasted_iota(jnp.int32, (n_win, LANES), 0)
        onehot[r] = jnp.where(ids == windows[r : r + 1, :], 1.0, 0.0).astype(F32)


    def take_piece(step):
        other, place = peer(step)
        pltpu.make_async_remote_copy(
            src_ref=own.at[0],
            dst_ref=parts.at[other],
            send_sem=send1.at[0],
            recv_sem=recv1.at[other],
            device_id=place,
            device_id_type=MESH,
        ).wait_recv()

    each(1, peers, take_piece)

    records = []
    for c in range(piece):
        for q in range(plane):
            total = parts[q * n_grp, c]
            for g in range(1, n_grp):
                total = total + parts[q * n_grp + g, c]
            records.append(total)
    for t in range(n_tx):
        for c in range(piece):
            value = jnp.zeros((n_win, LANES), F32)
            for q in range(plane):
                hit = jnp.full((n_win, LANES), acquirer[t], jnp.int32) == level * plane + q
                value = value + jnp.where(hit, records[c * plane + q], 0.0)
            line[level, t, c] = value
        for step in range(1, n_lines):
            other, place = along(step)
            copy = pltpu.make_async_remote_copy(
                src_ref=line.at[level, t],
                dst_ref=line.at[level, t],
                send_sem=send2.at[t, step],
                recv_sem=recv2.at[t, level],
                device_id=place,
                device_id_type=MESH,
            )
            copy.start()
            copies.append(copy)

    def share_copy(t, step, owner):
        other, place = peer(step)
        rows_of = pl.ds((me if owner is me else other) * piece, piece)
        return pltpu.make_async_remote_copy(
            src_ref=tables[t].at[rows_of],
            dst_ref=tables[t].at[rows_of],
            send_sem=send3.at[t, step],
            recv_sem=recv3.at[t, me if owner is me else other],
            device_id=place,
            device_id_type=MESH,
        )

    for t in range(n_tx):
        for step in range(1, n_lines):
            other, place = along(step)
            pltpu.make_async_remote_copy(
                src_ref=line.at[other, t],
                dst_ref=line.at[other, t],
                send_sem=send2.at[t, step],
                recv_sem=recv2.at[t, other],
                device_id=place,
                device_id_type=MESH,
            ).wait_recv()
        for c in range(piece):
            value = line[0, t, c]
            for l in range(1, n_lines):
                value = value + line[l, t, c]
            tables[t][me * piece + c] = jnp.concatenate(split_terms(value, 2), axis=0)
        each(1, peers, lambda step, t=t: share_copy(t, step, me).start())

    row_ids = lax.broadcasted_iota(jnp.int32, (row_blocks, LANES), 0)
    acc = jnp.zeros((row_blocks, LANES), F32)
    for t in range(n_tx):
        panel_loads[t].wait()
        each(1, peers, lambda step, t=t: share_copy(t, step, None).wait_recv())

        def some_slots(turn, acc, t=t):
            for pair in range(unroll // 2):
                first = turn * unroll + 2 * pair
                signals = [
                    tables[t][columns[t, 0, grp * width + first + i]] for i in range(2)
                ]
                both = lax.dot_general(
                    jnp.concatenate(signals, axis=0),
                    panels_v[t, pl.ds(first, 2)].reshape(2 * LANES, LANES),
                    (((1,), (1,)), ((), ())),
                    preferred_element_type=F32,
                )
                for i in range(2):
                    slot = grp * width + first + i
                    r = rows[t, 0, slot]
                    own_part = both[2 * n_win * i :, i * LANES : (i + 1) * LANES]
                    value = (own_part[:n_win] + own_part[n_win : 2 * n_win]) * onehot[r]
                    value = jnp.sum(value, axis=0, keepdims=True)
                    target = jnp.where(slot < counts[0, t], r, -1)
                    acc = acc + jnp.where(row_ids == target, value, 0.0)
            return acc

        acc = lax.fori_loop(0, width // unroll, some_slots, acc)

    sums[grp] = acc
    for step in range(1, n_grp):
        other, place = sibling(step)
        copy = pltpu.make_async_remote_copy(
            src_ref=sums.at[grp],
            dst_ref=sums.at[grp],
            send_sem=send4.at[step],
            recv_sem=recv4.at[grp],
            device_id=place,
            device_id_type=MESH,
        )
        copy.start()
        copies.append(copy)
    for step in range(1, n_grp):
        other, place = sibling(step)
        pltpu.make_async_remote_copy(
            src_ref=sums.at[other],
            dst_ref=sums.at[other],
            send_sem=send4.at[step],
            recv_sem=recv4.at[other],
            device_id=place,
            device_id_type=MESH,
        ).wait_recv()
    total = sums[0]
    for g in range(1, n_grp):
        total = total + sums[g]
    share = row_blocks // n_grp
    result = total[:share]
    for g in range(1, n_grp):
        result = jnp.where(grp == g, total[g * share : (g + 1) * share], result)
    image[...] = result
    for copy in copies:
        copy.wait_send()
    each(1, peers, lambda step: send_piece(step).wait_send())
    for t in range(n_tx):
        each(1, peers, lambda step, t=t: share_copy(t, step, me).wait_send())


def per_device(
    n_slab,
    n_grp,
    echo_data,
    acquirer,
    panels,
    block_count,
    block_rows,
    block_columns,
    apodization,
    window_index,
):
    channels, samples = echo_data.shape[1:]
    n_tx, width, block = panels.shape[1:4]
    n_win = apodization.shape[0]
    n_blocks = samples // block
    row_blocks = window_index.shape[0] // block
    plane = min(4, n_slab, n_blocks // n_grp)
    n_lines = n_slab // plane
    peers = plane * n_grp
    piece = n_blocks // peers
    assert block == LANES and piece * peers == n_blocks and plane * n_lines == n_slab
    unroll = min(16, width)
    dims = (n_grp, plane, n_lines, n_tx, n_win, piece, width, unroll)
    vmem = pl.BlockSpec(memory_space=pltpu.VMEM)
    hbm = pl.BlockSpec(memory_space=pltpu.HBM)
    dma = pltpu.SemaphoreType.DMA
    result = pl.pallas_call(
        functools.partial(kernel, dims),
        out_shape=jax.ShapeDtypeStruct((row_blocks // n_grp, LANES), F32),
        in_specs=[hbm] * 8,
        out_specs=vmem,
        scratch_shapes=[
            pltpu.VMEM(apodization.shape, F32),
            pltpu.VMEM((row_blocks, block), jnp.int32),
            pltpu.SMEM(acquirer.shape, jnp.int32),
            pltpu.SMEM(block_count.shape, jnp.int32),
            pltpu.SMEM((n_tx, 1, block_rows.shape[2]), jnp.int32),
            pltpu.SMEM((n_tx, 1, block_columns.shape[2]), jnp.int32),
            dma((6,)),
            pltpu.VMEM((peers, channels, piece * LANES), BF16),
            pltpu.VMEM((n_tx, width, block, block), BF16),
            pltpu.VMEM((peers, piece, n_win, LANES), F32),
            pltpu.VMEM((peers, piece, n_win, LANES), F32),
            pltpu.VMEM((n_lines, n_tx, piece, n_win, LANES), F32),
            [pltpu.VMEM((n_blocks, 2 * n_win, LANES), BF16)] * n_tx,
            pltpu.VMEM((row_blocks, n_win, LANES), F32),
            pltpu.VMEM((n_grp, row_blocks, LANES), F32),
            dma((peers,)),
            dma((n_tx,)),
            dma((peers,)),
            dma((peers,)),
            dma((n_tx, n_lines)),
            dma((n_tx, n_lines)),
            dma((n_tx, peers)),
            dma((n_tx, peers)),
            dma((n_grp,)),
            dma((n_grp,)),
        ],
        compiler_params=pltpu.CompilerParams(
            collective_id=0, has_side_effects=True, vmem_limit_bytes=62 * 1024 * 1024
        ),
        name="beamform",
    )(
        echo_data,
        panels,
        apodization,
        window_index.reshape(row_blocks, block),
        acquirer,
        block_count,
        block_rows.transpose(1, 0, 2),
        block_columns.transpose(1, 0, 2),
    )
    return result.reshape(-1)


def solution(mesh):
    return jax.shard_map(
        functools.partial(per_device, mesh.shape["slab"], mesh.shape["grp"]),
        mesh=mesh,
        in_specs=(
            P("slab", "grp", None),
            P(),
            P("slab", None, "grp", None, None),
            P("slab", None),
            P("slab", None, None),
            P("slab", None, None),
            P(None, "grp"),
            P("slab"),
        ),
        out_specs=P(("slab", "grp")),
        check_vma=False,
    )
```

```python
import functools

import jax
import jax.numpy as jnp
from jax import lax
from jax.experimental import pallas as pl
from jax.experimental.pallas import tpu as pltpu
from jax.sharding import PartitionSpec as P

MESH = pl.DeviceIdType.MESH
F32 = jnp.float32
BF16 = jnp.bfloat16
LANES = 128


def split_terms(x, n):
    terms = []
    for _ in range(n):
        term = x.astype(BF16)
        terms.append(term)
        x = x - term.astype(F32)
    return terms


def kernel(
    dims,
    echo,
    panels,
    apod_in,
    windows_in,
    acquirer_in,
    counts_in,
    rows_in,
    columns_in,
    image,
    apod,
    windows,
    acquirer,
    counts,
    rows,
    columns,
    small_sem,
    echo_v,
    panels_v,
    turned,
    own,
    parts,
    line,
    tables,
    onehot,
    sums,
    echo_sem,
    panel_sem,
    send1,
    recv1,
    send2,
    recv2,
    send3,
    recv3,
    send4,
    recv4,
):
    n_grp, plane, n_lines, n_tx, n_win, piece, width, unroll = dims
    peers = plane * n_grp
    span = piece * LANES
    slab, grp = lax.axis_index("slab"), lax.axis_index("grp")
    level, spot = slab // plane, slab % plane
    me = spot * n_grp + grp

    def peer(step):
        other = lax.rem(me + step, peers)
        return other, (level * plane + other // n_grp, lax.rem(other, n_grp))

    def along(step):
        other = lax.rem(level + step, n_lines)
        return other, (other * plane + spot, grp)

    def sibling(step):
        other = lax.rem(grp + step, n_grp)
        return other, (slab, other)

    barrier = pltpu.get_barrier_semaphore()
    for step in range(1, peers):
        pl.semaphore_signal(barrier, inc=1, device_id=peer(step)[1], device_id_type=MESH)
    for step in range(1, n_lines):
        pl.semaphore_signal(barrier, inc=1, device_id=along(step)[1], device_id_type=MESH)

    small = [
        pltpu.make_async_copy(source, target, small_sem.at[number])
        for number, (source, target) in enumerate(
            (
                (apod_in, apod),
                (acquirer_in, acquirer),
                (windows_in, windows),
                (counts_in, counts),
                (rows_in, rows),
                (columns_in, columns),
            )
        )
    ]
    small[0].start()
    order = [lax.rem(me + step, peers) for step in range(1, peers + 1)]
    loads = []
    for number, part in enumerate(order):
        cut = pl.ds(pl.multiple_of(part * span, span), span)
        load = pltpu.make_async_copy(echo.at[0, :, cut], echo_v.at[number], echo_sem.at[number])
        load.start()
        loads.append(load)
    panel_loads = []
    for t in range(n_tx):
        load = pltpu.make_async_copy(panels.at[0, t], panels_v.at[t], panel_sem.at[t])
        panel_loads.append(load)

    for load in small[1:]:
        load.start()

    small[0].wait()
    weights = jnp.concatenate(split_terms(apod[...], 3), axis=0)

    pl.semaphore_wait(barrier, peers - 1 + n_lines - 1)

    def turn_panels(t):
        panel_loads[t].wait()

        def two_pairs(turn, carry):
            for i in range(2):
                pair = 2 * turn + i
                for j in range(2):
                    turned[t, pair, :, j * LANES : (j + 1) * LANES] = panels_v[t, 2 * pair + j].T
            return carry

        lax.fori_loop(0, width // 4, two_pairs, 0)

    copies = []
    half = peers // 2
    for group in (range(half), range(half, peers)):
        for number in group:
            loads[number].wait()
        if group[-1] == peers - 1:
            for load in panel_loads:
                load.start()
        for number in group:
            terms = jnp.dot(weights, echo_v[number], preferred_element_type=F32)
            value = terms[:n_win] + terms[n_win : 2 * n_win] + terms[2 * n_win :]
            for c in range(piece):
                chunk = value[:, c * LANES : (c + 1) * LANES]
                if number == peers - 1:
                    parts[me, c] = chunk
                else:
                    own[number, c] = chunk
        for number in group:
            if number < peers - 1:
                copy = pltpu.make_async_remote_copy(
                    src_ref=own.at[number],
                    dst_ref=parts.at[me],
                    send_sem=send1.at[number],
                    recv_sem=recv1.at[me],
                    device_id=peer(number + 1)[1],
                    device_id_type=MESH,
                )
                copy.start()
                copies.append(copy)
    for load in small[1:]:
        load.wait()
    row_blocks = windows.shape[0]
    for r in range(row_blocks):
        ids = lax.broadcasted_iota(jnp.int32, (n_win, LANES), 0)
        onehot[r] = jnp.where(ids == windows[r : r + 1, :], 1.0, 0.0).astype(F32)

    turn_panels(0)
    for step in range(1, peers):
        other, place = peer(step)
        pltpu.make_async_remote_copy(
            src_ref=own.at[0],
            dst_ref=parts.at[other],
            send_sem=send1.at[0],
            recv_sem=recv1.at[other],
            device_id=place,
            device_id_type=MESH,
        ).wait_recv()

    records = []
    for c in range(piece):
        for q in range(plane):
            total = parts[q * n_grp, c]
            for g in range(1, n_grp):
                total = total + parts[q * n_grp + g, c]
            records.append(total)
    for t in range(n_tx):
        for c in range(piece):
            value = jnp.zeros((n_win, LANES), F32)
            for q in range(plane):
                hit = jnp.full((n_win, LANES), acquirer[t], jnp.int32) == level * plane + q
                value = value + jnp.where(hit, records[c * plane + q], 0.0)
            line[level, t, c] = value
        for step in range(1, n_lines):
            other, place = along(step)
            copy = pltpu.make_async_remote_copy(
                src_ref=line.at[level, t],
                dst_ref=line.at[level, t],
                send_sem=send2.at[t, step],
                recv_sem=recv2.at[t, level],
                device_id=place,
                device_id_type=MESH,
            )
            copy.start()
            copies.append(copy)

    turn_panels(1)

    mine = pl.ds(me * piece, piece)
    for t in range(n_tx):
        for step in range(1, n_lines):
            other, place = along(step)
            pltpu.make_async_remote_copy(
                src_ref=line.at[other, t],
                dst_ref=line.at[other, t],
                send_sem=send2.at[t, step],
                recv_sem=recv2.at[t, other],
                device_id=place,
                device_id_type=MESH,
            ).wait_recv()
        for c in range(piece):
            value = line[0, t, c]
            for l in range(1, n_lines):
                value = value + line[l, t, c]
            tables[t][me * piece + c] = jnp.concatenate(split_terms(value, 2), axis=0)
        for step in range(1, peers):
            other, place = peer(step)
            copy = pltpu.make_async_remote_copy(
                src_ref=tables[t].at[mine],
                dst_ref=tables[t].at[mine],
                send_sem=send3.at[t, step],
                recv_sem=recv3.at[t, me],
                device_id=place,
                device_id_type=MESH,
            )
            copy.start()
            copies.append(copy)

    row_ids = lax.broadcasted_iota(jnp.int32, (row_blocks, LANES), 0)
    acc = jnp.zeros((row_blocks, LANES), F32)
    for t in range(2, n_tx):
        turn_panels(t)
    for t in range(n_tx):
        for step in range(1, peers):
            other, place = peer(step)
            theirs = pl.ds(other * piece, piece)
            pltpu.make_async_remote_copy(
                src_ref=tables[t].at[theirs],
                dst_ref=tables[t].at[theirs],
                send_sem=send3.at[t, step],
                recv_sem=recv3.at[t, other],
                device_id=place,
                device_id_type=MESH,
            ).wait_recv()

        def some_slots(turn, acc, t=t):
            for pair in range(unroll // 2):
                first = turn * unroll + 2 * pair
                signals = [
                    tables[t][columns[t, 0, grp * width + first + i]] for i in range(2)
                ]
                both = jnp.dot(
                    jnp.concatenate(signals, axis=0),
                    turned[t, turn * (unroll // 2) + pair],
                    preferred_element_type=F32,
                )
                for i in range(2):
                    slot = grp * width + first + i
                    r = rows[t, 0, slot]
                    own_part = both[2 * n_win * i :, i * LANES : (i + 1) * LANES]
                    value = (own_part[:n_win] + own_part[n_win : 2 * n_win]) * onehot[r]
                    value = jnp.sum(value, axis=0, keepdims=True)
                    target = jnp.where(slot < counts[0, t], r, -1)
                    acc = acc + jnp.where(row_ids == target, value, 0.0)
            return acc

        acc = lax.fori_loop(0, width // unroll, some_slots, acc)

    sums[grp] = acc
    for step in range(1, n_grp):
        other, place = sibling(step)
        copy = pltpu.make_async_remote_copy(
            src_ref=sums.at[grp],
            dst_ref=sums.at[grp],
            send_sem=send4.at[step],
            recv_sem=recv4.at[grp],
            device_id=place,
            device_id_type=MESH,
        )
        copy.start()
        copies.append(copy)
    for step in range(1, n_grp):
        other, place = sibling(step)
        pltpu.make_async_remote_copy(
            src_ref=sums.at[other],
            dst_ref=sums.at[other],
            send_sem=send4.at[step],
            recv_sem=recv4.at[other],
            device_id=place,
            device_id_type=MESH,
        ).wait_recv()
    total = sums[0]
    for g in range(1, n_grp):
        total = total + sums[g]
    share = row_blocks // n_grp
    result = total[:share]
    for g in range(1, n_grp):
        result = jnp.where(grp == g, total[g * share : (g + 1) * share], result)
    image[...] = result
    for copy in copies:
        copy.wait_send()


def per_device(
    n_slab,
    n_grp,
    echo_data,
    acquirer,
    panels,
    block_count,
    block_rows,
    block_columns,
    apodization,
    window_index,
):
    channels, samples = echo_data.shape[1:]
    n_tx, width, block = panels.shape[1:4]
    n_win = apodization.shape[0]
    n_blocks = samples // block
    row_blocks = window_index.shape[0] // block
    plane = min(4, n_slab, n_blocks // n_grp)
    n_lines = n_slab // plane
    peers = plane * n_grp
    piece = n_blocks // peers
    assert block == LANES and piece * peers == n_blocks and plane * n_lines == n_slab
    unroll = min(16, width)
    dims = (n_grp, plane, n_lines, n_tx, n_win, piece, width, unroll)
    vmem = pl.BlockSpec(memory_space=pltpu.VMEM)
    hbm = pl.BlockSpec(memory_space=pltpu.HBM)
    dma = pltpu.SemaphoreType.DMA
    result = pl.pallas_call(
        functools.partial(kernel, dims),
        out_shape=jax.ShapeDtypeStruct((row_blocks // n_grp, LANES), F32),
        in_specs=[hbm] * 8,
        out_specs=vmem,
        scratch_shapes=[
            pltpu.VMEM(apodization.shape, F32),
            pltpu.VMEM((row_blocks, block), jnp.int32),
            pltpu.SMEM(acquirer.shape, jnp.int32),
            pltpu.SMEM(block_count.shape, jnp.int32),
            pltpu.SMEM((n_tx, 1, block_rows.shape[2]), jnp.int32),
            pltpu.SMEM((n_tx, 1, block_columns.shape[2]), jnp.int32),
            dma((6,)),
            pltpu.VMEM((peers, channels, piece * LANES), BF16),
            pltpu.VMEM((n_tx, width, block, block), BF16),
            pltpu.VMEM((n_tx, width // 2, block, 2 * block), BF16),
            pltpu.VMEM((peers, piece, n_win, LANES), F32),
            pltpu.VMEM((peers, piece, n_win, LANES), F32),
            pltpu.VMEM((n_lines, n_tx, piece, n_win, LANES), F32),
            [pltpu.VMEM((n_blocks, 2 * n_win, LANES), BF16)] * n_tx,
            pltpu.VMEM((row_blocks, n_win, LANES), F32),
            pltpu.VMEM((n_grp, row_blocks, LANES), F32),
            dma((peers,)),
            dma((n_tx,)),
            dma((peers,)),
            dma((peers,)),
            dma((n_tx, n_lines)),
            dma((n_tx, n_lines)),
            dma((n_tx, peers)),
            dma((n_tx, peers)),
            dma((n_grp,)),
            dma((n_grp,)),
        ],
        compiler_params=pltpu.CompilerParams(
            collective_id=0, has_side_effects=True, vmem_limit_bytes=62 * 1024 * 1024
        ),
        name="beamform",
    )(
        echo_data,
        panels,
        apodization,
        window_index.reshape(row_blocks, block),
        acquirer,
        block_count,
        block_rows.transpose(1, 0, 2),
        block_columns.transpose(1, 0, 2),
    )
    return result.reshape(-1)


def solution(mesh):
    return jax.shard_map(
        functools.partial(per_device, mesh.shape["slab"], mesh.shape["grp"]),
        mesh=mesh,
        in_specs=(
            P("slab", "grp", None),
            P(),
            P("slab", None, "grp", None, None),
            P("slab", None),
            P("slab", None, None),
            P("slab", None, None),
            P(None, "grp"),
            P("slab"),
        ),
        out_specs=P(("slab", "grp")),
        check_vma=False,
    )
```

```python
import functools

import jax
import jax.numpy as jnp
from jax import lax
from jax.experimental import pallas as pl
from jax.experimental.pallas import tpu as pltpu
from jax.sharding import PartitionSpec as P

MESH = pl.DeviceIdType.MESH
F32 = jnp.float32
BF16 = jnp.bfloat16
LANES = 128


def split_terms(x, n):
    terms = []
    for _ in range(n):
        term = x.astype(BF16)
        terms.append(term)
        x = x - term.astype(F32)
    return terms


def far_first(n):
    return sorted(range(1, n), key=lambda step: abs(2 * step - n))


def kernel(
    dims,
    echo,
    panels,
    apod_in,
    windows_in,
    acquirer_in,
    counts_in,
    rows_in,
    columns_in,
    image,
    apod,
    windows,
    acquirer,
    counts,
    rows,
    columns,
    small_sem,
    echo_v,
    panels_v,
    own,
    parts,
    line,
    tables,
    onehot,
    sums,
    echo_sem,
    panel_sem,
    send1,
    recv1,
    send2,
    recv2,
    send3,
    recv3,
    send4,
    recv4,
):
    n_grp, plane, n_lines, n_tx, n_win, piece, width, unroll = dims
    peers = plane * n_grp
    span = piece * LANES
    slab, grp = lax.axis_index("slab"), lax.axis_index("grp")
    level, spot = slab // plane, slab % plane
    me = spot * n_grp + grp

    def peer(step):
        other = lax.rem(me + step, peers)
        return other, (level * plane + other // n_grp, lax.rem(other, n_grp))

    def along(step):
        other = lax.rem(level + step, n_lines)
        return other, (other * plane + spot, grp)

    def sibling(step):
        other = lax.rem(grp + step, n_grp)
        return other, (slab, other)

    barrier = pltpu.get_barrier_semaphore()
    for step in range(1, peers):
        pl.semaphore_signal(barrier, inc=1, device_id=peer(step)[1], device_id_type=MESH)
    for step in range(1, n_lines):
        pl.semaphore_signal(barrier, inc=1, device_id=along(step)[1], device_id_type=MESH)

    small = [
        pltpu.make_async_copy(source, target, small_sem.at[number])
        for number, (source, target) in enumerate(
            (
                (apod_in, apod),
                (acquirer_in, acquirer),
                (windows_in, windows),
                (counts_in, counts),
                (rows_in, rows),
                (columns_in, columns),
            )
        )
    ]
    small[0].start()
    order = [lax.rem(me + step, peers) for step in range(1, peers + 1)]
    loads = []
    for number, part in enumerate(order):
        cut = pl.ds(pl.multiple_of(part * span, span), span)
        load = pltpu.make_async_copy(echo.at[0, :, cut], echo_v.at[number], echo_sem.at[number])
        load.start()
        loads.append(load)
    panel_loads = []
    for t in range(n_tx):
        load = pltpu.make_async_copy(panels.at[0, t], panels_v.at[t], panel_sem.at[t])
        panel_loads.append(load)

    for load in small[1:]:
        load.start()

    small[0].wait()
    weights = jnp.concatenate(split_terms(apod[...], 3), axis=0)

    copies = []
    half = peers // 2
    for group in (range(half), range(half, peers)):
        for number in group:
            loads[number].wait()
        if group[-1] == peers - 1:
            for load in panel_loads:
                load.start()
        for number in group:
            terms = jnp.dot(weights, echo_v[number], preferred_element_type=F32)
            value = terms[:n_win] + terms[n_win : 2 * n_win] + terms[2 * n_win :]
            for c in range(piece):
                chunk = value[:, c * LANES : (c + 1) * LANES]
                if number == peers - 1:
                    parts[me, c] = chunk
                else:
                    own[number, c] = chunk
        if group[0] == 0:
            pl.semaphore_wait(barrier, peers - 1 + n_lines - 1)
        for number in group:
            if number < peers - 1:
                copy = pltpu.make_async_remote_copy(
                    src_ref=own.at[number],
                    dst_ref=parts.at[me],
                    send_sem=send1.at[number],
                    recv_sem=recv1.at[me],
                    device_id=peer(number + 1)[1],
                    device_id_type=MESH,
                )
                copy.start()
                copies.append(copy)
    for load in small[1:]:
        load.wait()
    row_blocks = windows.shape[0]
    for r in range(row_blocks):
        ids = lax.broadcasted_iota(jnp.int32, (n_win, LANES), 0)
        onehot[r] = jnp.where(ids == windows[r : r + 1, :], 1.0, 0.0).astype(F32)

    for step in range(1, peers):
        other, place = peer(step)
        pltpu.make_async_remote_copy(
            src_ref=own.at[0],
            dst_ref=parts.at[other],
            send_sem=send1.at[0],
            recv_sem=recv1.at[other],
            device_id=place,
            device_id_type=MESH,
        ).wait_recv()

    records = []
    for c in range(piece):
        for q in range(plane):
            total = parts[q * n_grp, c]
            for g in range(1, n_grp):
                total = total + parts[q * n_grp + g, c]
            records.append(total)
    for t in range(n_tx):
        for c in range(piece):
            value = jnp.zeros((n_win, LANES), F32)
            for q in range(plane):
                hit = jnp.full((n_win, LANES), acquirer[t], jnp.int32) == level * plane + q
                value = value + jnp.where(hit, records[c * plane + q], 0.0)
            line[level, t, c] = value
        for step in range(1, n_lines):
            other, place = along(step)
            copy = pltpu.make_async_remote_copy(
                src_ref=line.at[level, t],
                dst_ref=line.at[level, t],
                send_sem=send2.at[t, step],
                recv_sem=recv2.at[t, level],
                device_id=place,
                device_id_type=MESH,
            )
            copy.start()
            copies.append(copy)

    mine = pl.ds(me * piece, piece)
    for t in range(n_tx):
        for step in range(1, n_lines):
            other, place = along(step)
            pltpu.make_async_remote_copy(
                src_ref=line.at[other, t],
                dst_ref=line.at[other, t],
                send_sem=send2.at[t, step],
                recv_sem=recv2.at[t, other],
                device_id=place,
                device_id_type=MESH,
            ).wait_recv()
        for c in range(piece):
            value = line[0, t, c]
            for l in range(1, n_lines):
                value = value + line[l, t, c]
            tables[t][me * piece + c] = jnp.concatenate(split_terms(value, 2), axis=0)
        for step in far_first(peers):
            other, place = peer(step)
            copy = pltpu.make_async_remote_copy(
                src_ref=tables[t].at[mine],
                dst_ref=tables[t].at[mine],
                send_sem=send3.at[t, step],
                recv_sem=recv3.at[t, me],
                device_id=place,
                device_id_type=MESH,
            )
            copy.start()
            copies.append(copy)

    row_ids = lax.broadcasted_iota(jnp.int32, (row_blocks, LANES), 0)
    acc = jnp.zeros((row_blocks, LANES), F32)
    for t in range(n_tx):
        panel_loads[t].wait()
        for step in range(1, peers):
            other, place = peer(step)
            theirs = pl.ds(other * piece, piece)
            pltpu.make_async_remote_copy(
                src_ref=tables[t].at[theirs],
                dst_ref=tables[t].at[theirs],
                send_sem=send3.at[t, step],
                recv_sem=recv3.at[t, other],
                device_id=place,
                device_id_type=MESH,
            ).wait_recv()

        def some_slots(turn, acc, t=t):
            for pair in range(unroll // 2):
                first = turn * unroll + 2 * pair
                signals = [
                    tables[t][columns[t, 0, grp * width + first + i]] for i in range(2)
                ]
                both = lax.dot_general(
                    jnp.concatenate(signals, axis=0),
                    panels_v[t, pl.ds(first, 2)].reshape(2 * LANES, LANES),
                    (((1,), (1,)), ((), ())),
                    preferred_element_type=F32,
                )
                for i in range(2):
                    slot = grp * width + first + i
                    r = rows[t, 0, slot]
                    own_part = both[2 * n_win * i :, i * LANES : (i + 1) * LANES]
                    value = (own_part[:n_win] + own_part[n_win : 2 * n_win]) * onehot[r]
                    value = jnp.sum(value, axis=0, keepdims=True)
                    target = jnp.where(slot < counts[0, t], r, -1)
                    acc = acc + jnp.where(row_ids == target, value, 0.0)
            return acc

        acc = lax.fori_loop(0, width // unroll, some_slots, acc)

    sums[grp] = acc
    for step in range(1, n_grp):
        other, place = sibling(step)
        copy = pltpu.make_async_remote_copy(
            src_ref=sums.at[grp],
            dst_ref=sums.at[grp],
            send_sem=send4.at[step],
            recv_sem=recv4.at[grp],
            device_id=place,
            device_id_type=MESH,
        )
        copy.start()
        copies.append(copy)
    for step in range(1, n_grp):
        other, place = sibling(step)
        pltpu.make_async_remote_copy(
            src_ref=sums.at[other],
            dst_ref=sums.at[other],
            send_sem=send4.at[step],
            recv_sem=recv4.at[other],
            device_id=place,
            device_id_type=MESH,
        ).wait_recv()
    total = sums[0]
    for g in range(1, n_grp):
        total = total + sums[g]
    share = row_blocks // n_grp
    result = total[:share]
    for g in range(1, n_grp):
        result = jnp.where(grp == g, total[g * share : (g + 1) * share], result)
    image[...] = result
    for copy in copies:
        copy.wait_send()


def per_device(
    n_slab,
    n_grp,
    echo_data,
    acquirer,
    panels,
    block_count,
    block_rows,
    block_columns,
    apodization,
    window_index,
):
    channels, samples = echo_data.shape[1:]
    n_tx, width, block = panels.shape[1:4]
    n_win = apodization.shape[0]
    n_blocks = samples // block
    row_blocks = window_index.shape[0] // block
    plane = min(4, n_slab, n_blocks // n_grp)
    n_lines = n_slab // plane
    peers = plane * n_grp
    piece = n_blocks // peers
    assert block == LANES and piece * peers == n_blocks and plane * n_lines == n_slab
    unroll = min(16, width)
    dims = (n_grp, plane, n_lines, n_tx, n_win, piece, width, unroll)
    vmem = pl.BlockSpec(memory_space=pltpu.VMEM)
    hbm = pl.BlockSpec(memory_space=pltpu.HBM)
    dma = pltpu.SemaphoreType.DMA
    result = pl.pallas_call(
        functools.partial(kernel, dims),
        out_shape=jax.ShapeDtypeStruct((row_blocks // n_grp, LANES), F32),
        in_specs=[hbm] * 8,
        out_specs=vmem,
        scratch_shapes=[
            pltpu.VMEM(apodization.shape, F32),
            pltpu.VMEM((row_blocks, block), jnp.int32),
            pltpu.SMEM(acquirer.shape, jnp.int32),
            pltpu.SMEM(block_count.shape, jnp.int32),
            pltpu.SMEM((n_tx, 1, block_rows.shape[2]), jnp.int32),
            pltpu.SMEM((n_tx, 1, block_columns.shape[2]), jnp.int32),
            dma((6,)),
            pltpu.VMEM((peers, channels, piece * LANES), BF16),
            pltpu.VMEM((n_tx, width, block, block), BF16),
            pltpu.VMEM((peers, piece, n_win, LANES), F32),
            pltpu.VMEM((peers, piece, n_win, LANES), F32),
            pltpu.VMEM((n_lines, n_tx, piece, n_win, LANES), F32),
            [pltpu.VMEM((n_blocks, 2 * n_win, LANES), BF16)] * n_tx,
            pltpu.VMEM((row_blocks, n_win, LANES), F32),
            pltpu.VMEM((n_grp, row_blocks, LANES), F32),
            dma((peers,)),
            dma((n_tx,)),
            dma((peers,)),
            dma((peers,)),
            dma((n_tx, n_lines)),
            dma((n_tx, n_lines)),
            dma((n_tx, peers)),
            dma((n_tx, peers)),
            dma((n_grp,)),
            dma((n_grp,)),
        ],
        compiler_params=pltpu.CompilerParams(
            collective_id=0, has_side_effects=True, vmem_limit_bytes=62 * 1024 * 1024
        ),
        name="beamform",
    )(
        echo_data,
        panels,
        apodization,
        window_index.reshape(row_blocks, block),
        acquirer,
        block_count,
        block_rows.transpose(1, 0, 2),
        block_columns.transpose(1, 0, 2),
    )
    return result.reshape(-1)


def solution(mesh):
    return jax.shard_map(
        functools.partial(per_device, mesh.shape["slab"], mesh.shape["grp"]),
        mesh=mesh,
        in_specs=(
            P("slab", "grp", None),
            P(),
            P("slab", None, "grp", None, None),
            P("slab", None),
            P("slab", None, None),
            P("slab", None, None),
            P(None, "grp"),
            P("slab"),
        ),
        out_specs=P(("slab", "grp")),
        check_vma=False,
    )
```
